32 devices in a mesh: groups: 2 (over x), dp: 4 (over z), tensor: 4 (over y, core).
Axes of the slice: x: 2, y: 2, z: 4, core: 2. Of those that a mesh axis runs over, the one named last changes fastest.
Arguments:
- queries: bfloat16 [4096, 8192], P(('groups', 'dp'), 'tensor'), parts along dimension 0, may hold values from -8 to 8
- suffix_rotated_key_slots: bfloat16 [4096, 1024], P(('groups', 'dp'), 'tensor'), parts along dimension 0, may hold values from -8 to 8, as said below
- suffix_value_slots: bfloat16 [4096, 1024], P(('groups', 'dp'), 'tensor'), parts along dimension 0, may hold values from -8 to 8, as said below
- shared_prefix_key_slots: bfloat16 [4096, 1024], P(('groups', 'dp'), 'tensor'), parts along dimension 0, may hold values from -8 to 8, as said below
- shared_prefix_value_slots: bfloat16 [4096, 1024], P(('groups', 'dp'), 'tensor'), parts along dimension 0, may hold values from -8 to 8, as said below
- lengths: int32 [8, 4], P(('groups', 'dp')), parts along dimension 0, may hold values from 1 to 256, 512 in all within a row
- request_adapter_index: int32 [8, 4], P(('groups', 'dp')), parts along dimension 0, may hold values from 0 to 63
- output_weight_matrix: bfloat16 [8192, 8192], P('tensor'), may hold values from -0.5 to 0.5
- adapter_down_factors: bfloat16 [64, 8192, 64], P('dp', 'tensor'), may hold values from -0.5 to 0.5
- adapter_up_factors: bfloat16 [64, 64, 8192], P('dp', None, 'tensor'), may hold values from -0.75 to 0.75
Outputs:
- projected: bfloat16 [4096, 8192], P(('groups', 'dp'), 'tensor'), parts along dimension 0
The draws below stay inside these ranges and needn't reach their ends.
There are 2 independent parts, one for each index of `groups`. The reference program is written for one: setup_inputs(seed, part) draws one part's arguments, and reference() takes and returns one part's arrays. A program takes and returns all parts, laid end to end along the dimension named above; an argument that names none is the same for every part. Nothing has to cross between parts.
Inputs may be any that keep to these rules, and one draw needn't show every extreme that they name: `shared_prefix_key_slots`: cache slot s holds key-value head s * 1; slots of the same head are equal. `shared_prefix_value_slots`: cache slot s holds key-value head s * 1; slots of the same head are equal. `suffix_rotated_key_slots`: cache slot s holds key-value head s * 1; slots of the same head are equal. `suffix_value_slots`: cache slot s holds key-value head s * 1; slots of the same head are equal.
All inputs are finite; a program needn't handle non-finite values.
Results may differ from the reference program's by a relative error of at most 0.014.
Values may be sent and summed in bfloat16 or wider, within the bound.
No kernel may reach another device: no remote copies, remote signals or barrier semaphores. Data moves between devices by JAX's collectives and lax.ppermute only.
A program may use at most 320 MiB of HBM per device.

```python
import math
import jax
import jax.numpy as jnp
import numpy as np
from jax import lax

MODEL_WIDTH = 8192
H = 64
KVH = 8
HD = 128
ADAPTER_RANK = 64
ADAPTER_COUNT = 64
REQ_DEV = 4
TOK_DEV = 512
TOKENS = 2048
PREFIX = 2048
KVS = 8
N_DP = 4


def spread_slots(heads):
    slot_head = jnp.arange(KVS) * KVH // KVS
    return heads[:, slot_head, :].reshape(heads.shape[0], KVS * HD)


def draw_queries(key, part):
    key = jax.random.fold_in(key, 11)
    field = jnp.clip(jax.random.normal(key, (TOKENS, MODEL_WIDTH), jnp.float32), -8.0, 8.0)
    return field.astype(jnp.bfloat16)


def draw_shared_prefix_key_slots(key, part):
    key = jax.random.fold_in(key, 12)
    heads = jnp.clip(jax.random.normal(key, (PREFIX, KVH, HD), jnp.float32), -8.0, 8.0)
    return spread_slots(heads).astype(jnp.bfloat16)


def draw_shared_prefix_value_slots(key, part):
    key = jax.random.fold_in(key, 13)
    heads = jnp.clip(jax.random.normal(key, (PREFIX, KVH, HD), jnp.float32), -8.0, 8.0)
    return spread_slots(heads).astype(jnp.bfloat16)


def draw_suffix_rotated_key_slots(key, part):
    key = jax.random.fold_in(key, 14)
    heads = jnp.clip(jax.random.normal(key, (TOKENS, KVH, HD), jnp.float32), -8.0, 8.0)
    return spread_slots(heads).astype(jnp.bfloat16)


def draw_suffix_value_slots(key, part):
    key = jax.random.fold_in(key, 15)
    heads = jnp.clip(jax.random.normal(key, (TOKENS, KVH, HD), jnp.float32), -8.0, 8.0)
    return spread_slots(heads).astype(jnp.bfloat16)


def touch_ends(result, stream_key, low, largest):
    place = [jax.random.randint(jax.random.fold_in(stream_key, axis), (), 0, length) for axis, length in enumerate(result.shape)]
    main_axis = result.shape.index(max(result.shape))
    beside = place[:main_axis] + [(place[main_axis] + 1) % result.shape[main_axis]] + place[main_axis + 1:]
    return result.at[tuple(place)].set(low).at[tuple(beside)].set(largest)


def block_levels(key, shape, pieces, least, top_value):
    def one(dim, blocks):
        heights = jax.random.uniform(jax.random.fold_in(jax.random.fold_in(key, 6), dim), (blocks,), jnp.float32, least / len(pieces), top_value / len(pieces))
        return jnp.repeat(jnp.exp(heights), shape[dim] // blocks).reshape((-1,) + (1,) * (len(shape) - dim - 1))

    factor_of = one(*pieces[0])
    for cut in pieces[1:]:
        factor_of = factor_of * one(*cut)
    return factor_of


def profile(number_of, total, limit, slope):
    portions = [(1 << 20) // math.isqrt(grade ** slope) + 1 for grade in range(2, number_of + 1)]
    surplus, counts = total - limit - (number_of - 1), [1] * (number_of - 1)
    while surplus > 0:
        movable = [i for i in range(number_of - 1) if counts[i] < limit]
        whole, remaining = sum([portions[i] for i in movable]), surplus
        for i in movable:
            more = min(limit - counts[i], max(1, remaining * portions[i] // whole), surplus)
            counts[i] = counts[i] + more
            surplus = surplus - more
    return np.array([limit] + counts)


def uneven_parts(rng, amount, total, bound, skew):
    if amount == 2:
        one = jax.random.randint(rng, (), max(1, total - bound), min(bound, total - 1) + 1)
        return jnp.stack([one, total - one])
    sizes = jnp.asarray(profile(amount, total, bound, skew), jnp.int32)
    couples = (amount - 1) // 2
    source_of, taker = sizes[1:1 + 2 * couples:2], sizes[2:2 + 2 * couples:2]
    margin = jnp.minimum(source_of - 1, bound - taker)
    shifted = jax.random.randint(jax.random.fold_in(rng, 1), (couples,), 0, 1 << 20) % (margin + 1)
    sizes = sizes.at[1:1 + 2 * couples:2].set(source_of - shifted).at[2:2 + 2 * couples:2].set(taker + shifted)
    return sizes[jax.random.permutation(jax.random.fold_in(rng, 2), amount)]


def bell_draw(rng, shape, width, limit, split=(), held_as=jnp.bfloat16):
    drawn = width * jax.random.normal(rng, shape, jnp.float32)
    if split:
        drawn = drawn * block_levels(rng, shape, split, -0.22, 0.18)
    return jnp.clip(drawn, -limit, limit).astype(held_as)


def setup_inputs(seed: int = 0, part: int = 0) -> dict:
    splits = jax.random.split(jax.random.key(seed), 11)
    part_splits = jax.random.split(jax.random.fold_in(splits[10], part), 11)
    queries = draw_queries(jax.random.fold_in(jax.random.fold_in(splits[10], part), 71), part)
    suffix_rotated_key_slots = draw_suffix_rotated_key_slots(jax.random.fold_in(jax.random.fold_in(splits[10], part), 71), part)
    suffix_value_slots = draw_suffix_value_slots(jax.random.fold_in(jax.random.fold_in(splits[10], part), 71), part)
    shared_prefix_key_slots = draw_shared_prefix_key_slots(jax.random.fold_in(jax.random.fold_in(splits[10], part), 71), part)
    shared_prefix_value_slots = draw_shared_prefix_value_slots(jax.random.fold_in(jax.random.fold_in(splits[10], part), 71), part)
    lengths = jax.vmap(lambda own: uneven_parts(own, REQ_DEV, TOK_DEV, TOK_DEV // 2, 2))(jax.random.split(part_splits[5], N_DP)).reshape((N_DP, REQ_DEV)).astype(jnp.int32)
    request_adapter_index = touch_ends(jax.random.randint(part_splits[6], (N_DP, REQ_DEV), 0, ADAPTER_COUNT), jax.random.fold_in(part_splits[6], 1), 0, ADAPTER_COUNT - 1).astype(jnp.int32)
    output_weight_matrix = bell_draw(splits[7], (MODEL_WIDTH, MODEL_WIDTH), (MODEL_WIDTH // 64) ** -0.5, 0.5, ((0, 4),))
    adapter_down_factors = bell_draw(splits[8], (ADAPTER_COUNT, MODEL_WIDTH, ADAPTER_RANK), (MODEL_WIDTH // 64) ** -0.5, 0.5, ((0, 4), (1, 4)))
    adapter_up_factors = bell_draw(splits[9], (ADAPTER_COUNT, ADAPTER_RANK, MODEL_WIDTH), ADAPTER_RANK ** -0.5, 0.75, ((0, 4), (2, 4)))
    return dict(queries=queries, suffix_rotated_key_slots=suffix_rotated_key_slots, suffix_value_slots=suffix_value_slots, shared_prefix_key_slots=shared_prefix_key_slots, shared_prefix_value_slots=shared_prefix_value_slots, lengths=lengths, request_adapter_index=request_adapter_index, output_weight_matrix=output_weight_matrix, adapter_down_factors=adapter_down_factors, adapter_up_factors=adapter_up_factors)


def reference(queries, suffix_rotated_key_slots, suffix_value_slots, shared_prefix_key_slots, shared_prefix_value_slots, lengths, request_adapter_index, output_weight_matrix, adapter_down_factors, adapter_up_factors):
    group_size = H // KVS
    score_scale = 1.0 / math.sqrt(HD)
    prefix_key_heads = shared_prefix_key_slots.reshape(PREFIX, KVS, HD).astype(jnp.float32)
    prefix_value_heads = shared_prefix_value_slots.reshape(PREFIX, KVS, HD).astype(jnp.float32)
    position = jnp.arange(TOK_DEV, dtype=jnp.int32)
    request_ids = jnp.arange(REQ_DEV, dtype=jnp.int32)

    def one_block(index):
        first_row = index * TOK_DEV
        query_block = lax.dynamic_slice_in_dim(queries, first_row, TOK_DEV, 0).reshape(TOK_DEV, KVS, group_size, HD).astype(jnp.float32)
        key_block = lax.dynamic_slice_in_dim(suffix_rotated_key_slots, first_row, TOK_DEV, 0).reshape(TOK_DEV, KVS, HD).astype(jnp.float32)
        value_block = lax.dynamic_slice_in_dim(suffix_value_slots, first_row, TOK_DEV, 0).reshape(TOK_DEV, KVS, HD).astype(jnp.float32)
        block_lengths = lax.dynamic_index_in_dim(lengths, index, 0, keepdims=False)
        seg_ends = jnp.cumsum(block_lengths).astype(jnp.int32)
        request_of = lax.optimization_barrier(jnp.sum((position[:, None] >= seg_ends[None, :]).astype(jnp.int32), axis=1))
        allowed_suffix = (request_of[:, None] == request_of[None, :]) & (position[None, :] <= position[:, None])
        allowed = jnp.concatenate([jnp.ones((TOK_DEV, PREFIX), dtype=bool), allowed_suffix], axis=1)

        def one_slot(slot):
            query_slot = lax.dynamic_index_in_dim(query_block, slot, 1, keepdims=False)
            key_all = jnp.concatenate([lax.dynamic_index_in_dim(prefix_key_heads, slot, 1, keepdims=False), lax.dynamic_index_in_dim(key_block, slot, 1, keepdims=False)], axis=0)
            value_all = jnp.concatenate([lax.dynamic_index_in_dim(prefix_value_heads, slot, 1, keepdims=False), lax.dynamic_index_in_dim(value_block, slot, 1, keepdims=False)], axis=0)
            scores = jnp.einsum('tgd,kd->gtk', query_slot, key_all) * score_scale
            scores = jnp.where(allowed[None], scores, -1e+30)
            peak = lax.optimization_barrier(jnp.max(scores, axis=-1, keepdims=True))
            weights = jnp.exp(scores - peak)
            totals = lax.optimization_barrier(jnp.sum(weights, axis=-1))
            weighted = jnp.einsum('gtk,kd->tgd', weights.astype(jnp.bfloat16).astype(jnp.float32), value_all)
            return weighted / jnp.transpose(totals, (1, 0))[:, :, None]
        slot_outputs = lax.map(one_slot, jnp.arange(KVS, dtype=jnp.int32))
        attended_block = jnp.transpose(slot_outputs, (1, 0, 2, 3)).reshape(TOK_DEV, MODEL_WIDTH).astype(jnp.bfloat16)
        select = (request_of[:, None] == request_ids[None, :]).astype(jnp.float32)
        block_numbers = lax.dynamic_index_in_dim(request_adapter_index, index, 0, keepdims=False)
        picked_down_factors = adapter_down_factors[block_numbers].astype(jnp.float32)
        picked_up_factors = adapter_up_factors[block_numbers].astype(jnp.float32)
        first_products = jnp.einsum('tk,rkq->trq', attended_block.astype(jnp.float32), picked_down_factors)
        shrink = lax.optimization_barrier(jnp.sum(first_products * select[:, :, None], axis=1)).astype(jnp.bfloat16)
        spread_shrink = select[:, :, None] * shrink.astype(jnp.float32)[:, None, :]
        expand = jnp.einsum('trq,rqd->td', spread_shrink, picked_up_factors)
        base = jnp.dot(attended_block, output_weight_matrix, preferred_element_type=jnp.float32)
        return (base + expand).astype(jnp.bfloat16)
    blocks = lax.map(one_block, jnp.arange(N_DP, dtype=jnp.int32))
    return blocks.reshape(TOKENS, MODEL_WIDTH)
```

```python
import functools
import math

import jax
import jax.numpy as jnp
from jax import lax
from jax.experimental import pallas as pl
from jax.experimental.pallas import tpu as pltpu
from jax.sharding import PartitionSpec as P

HD = 128
LAG = 2
ROUNDS = 6
CHUNKS = 2
F32 = jnp.float32
BF16 = jnp.bfloat16
SMEM = pltpu.MemorySpace.SMEM
VMEM = pltpu.MemorySpace.VMEM


def params(mib=32, **more):
    return pltpu.CompilerParams(vmem_limit_bytes=mib * 1024 * 1024, **more)


def attend_kernel(blocks, rows, scale, q_ref, seg_q, seg_k, *refs):
    keys, values = refs[: blocks + 1], refs[blocks + 1 : 2 * blocks + 2]
    out_ref, bias = refs[-2], refs[-1]

    @pl.when(pl.program_id(0) == 0)
    def _():
        same = seg_q[:, 0:1] == seg_k[0:1, :]
        first = seg_q[:, 1:2]
        where_k = lax.broadcasted_iota(jnp.int32, bias.shape, 1)
        bias[...] = jnp.where(same & (where_k <= first), 0.0, -1e30)

    q = q_ref[...]
    dims = (((1,), (1,)), ((), ()))
    scores = [lax.dot_general(q, k[...], dims, preferred_element_type=F32) for k in keys]
    scores[0] = scores[0] + bias[...]
    peak = functools.reduce(jnp.maximum, [jnp.max(s, axis=1, keepdims=True) for s in scores])
    factor = scale * math.log2(math.e)
    total = jnp.zeros((q.shape[0], 1), F32)
    summed = jnp.zeros((q.shape[0], HD), F32)
    for s, v in zip(scores, values):
        w = jnp.exp2((s - peak) * factor)
        total = total + jnp.sum(w, axis=1, keepdims=True)
        summed = summed + jnp.dot(w.astype(BF16), v[...], preferred_element_type=F32)
    out_ref[...] = (summed / total).astype(BF16)


def attend(q, seg_q, seg_k, keys, values, chunk, chunks):
    tokens, width = q.shape
    rows = tokens // chunks
    heads, slots = width // HD, keys[0].shape[1] // HD
    group = heads // slots
    blocks = len(keys) - 1
    kv_specs = [pl.BlockSpec((k.shape[0], HD), lambda h: (0, h // group)) for k in keys]
    n_keys = sum(k.shape[0] for k in keys)
    return pl.pallas_call(
        functools.partial(attend_kernel, blocks, rows, 1.0 / math.sqrt(HD)),
        grid=(heads,),
        out_shape=jax.ShapeDtypeStruct((rows, width), BF16),
        in_specs=[
            pl.BlockSpec((rows, HD), lambda h: (chunk, h)),
            pl.BlockSpec((rows, 2), lambda h: (chunk, 0)),
            pl.BlockSpec((1, tokens), lambda h: (0, 0)),
            *kv_specs,
            *kv_specs,
        ],
        out_specs=pl.BlockSpec((rows, HD), lambda h: (0, h)),
        scratch_shapes=[pltpu.VMEM((rows, tokens), F32)],
        compiler_params=params(40),
        cost_estimate=pl.CostEstimate(
            flops=8 * rows * n_keys * width, bytes_accessed=4 * rows * width, transcendentals=0
        ),
        name="attend",
    )(q, seg_q, seg_k, *keys, *values)


def project_kernel(which, a_ref, w_ref, out_ref):
    out_ref[...] = jnp.dot(a_ref[...], w_ref[...], preferred_element_type=F32).astype(BF16)


def project(a, w, block, count):
    rows, depth = a.shape
    wide = w.shape[1] // count
    tile = min(512, wide)
    steps = wide // tile
    return pl.pallas_call(
        project_kernel,
        out_shape=jax.ShapeDtypeStruct((rows, wide), BF16),
        grid_spec=pltpu.PrefetchScalarGridSpec(
            num_scalar_prefetch=1,
            grid=(steps,),
            in_specs=[
                pl.BlockSpec((rows, depth), lambda j, which: (0, 0)),
                pl.BlockSpec((depth, tile), lambda j, which: (0, which[0] * steps + j)),
            ],
            out_specs=pl.BlockSpec((rows, tile), lambda j, which: (0, j)),
        ),
        compiler_params=params(24),
        cost_estimate=pl.CostEstimate(
            flops=2 * rows * depth * wide, bytes_accessed=2 * depth * wide, transcendentals=0
        ),
        name="project",
    )(block, a, w)


def most_rounds(n_dp, requests):
    return requests * (n_dp - 1) + LAG * n_dp


def schedule_kernel(n_dp, requests, per, idx_ref, z_ref, out_ref):
    limit = most_rounds(n_dp, requests)
    idx = idx_ref[...]
    shape = idx.shape
    z = z_ref[0]
    lane = lax.broadcasted_iota(jnp.int32, shape, 1)
    row = lax.broadcasted_iota(jnp.int32, shape, 0)
    valid = (lane < n_dp * requests) & (row < 4)
    down = (row % 2) == 1
    taker = lane // requests
    holder = idx // per
    local = idx % per
    own = valid & (taker == holder)
    dst = jnp.where(down, n_dp - 1 - taker, taker)
    src = jnp.where(down, n_dp - 1 - holder, holder)
    me = jnp.where(down, n_dp - 1 - z, z)
    moving = valid & (src < dst)
    dst = jnp.where(moving, dst, 0)
    pos = jnp.where(moving, src, 0)
    zero = jnp.zeros(shape, jnp.int32)

    def one_round(carry):
        k, _, pos, ready, came, codes = carry
        sent_code = zero
        for link in range(n_dp - 1):
            can = (pos == link) & (dst > link) & (ready <= k)
            key = jnp.where(can, dst * 256 + 255 - lane, -1)
            best = jnp.max(key, axis=1, keepdims=True)
            chosen = can & (key == best)
            code = jnp.where(src == me, local, per + came)
            sent_code = jnp.where(chosen & (me == link), code, sent_code)
            came = jnp.where(chosen & (me == link + 1), k, came)
            pos = jnp.where(chosen, link + 1, pos)
            ready = jnp.where(chosen, k + LAG, ready)
        total = jnp.sum(sent_code, axis=1, keepdims=True)
        codes = jnp.where(lane == k, total, codes)
        left = jnp.max(jnp.where(pos < dst, 1, 0))
        return k + 1, left, pos, ready, came, codes

    first = jnp.max(jnp.where(pos < dst, 1, 0))
    rounds, _, _, _, came, codes = lax.while_loop(
        lambda c: (c[1] > 0) & (c[0] < limit), one_round, (jnp.int32(0), first, pos, zero, zero, zero)
    )
    place = jnp.where(own & (row == 0), local, 0)
    place = place + jnp.where(moving & (row == 0), per + came, 0)
    place = place + jnp.where(moving & (row == 1), per + limit + came, 0)
    place = jnp.sum(jnp.where(row < 2, place, 0), axis=0, keepdims=True)
    out = jnp.where(row < 2, codes, 0)
    out = jnp.where(row == 2, place, out)
    out_ref[...] = jnp.where(row == 3, rounds, out)


def make_schedule(n_dp, requests, per, idx_rows, z):
    return pl.pallas_call(
        functools.partial(schedule_kernel, n_dp, requests, per),
        out_shape=jax.ShapeDtypeStruct((8, 128), jnp.int32),
        in_specs=[pl.BlockSpec(memory_space=VMEM), pl.BlockSpec(memory_space=SMEM)],
        out_specs=pl.BlockSpec(memory_space=VMEM),
        name="schedule",
    )(idx_rows, z)


def fetch(code, per, own, ups, downs, limit, out, sem):
    @pl.when(code < per)
    def _():
        pltpu.make_async_copy(own.at[jnp.minimum(code, per - 1)], out, sem).start()

    for base, came in ((per, ups), (per + limit, downs)):
        for k, ref in enumerate(came):

            @pl.when(code == base + k)
            def _(ref=ref):
                pltpu.make_async_copy(ref, out, sem).start()


def pick_kernel(first, count, per, limit, n_up, n_down, sched, own, *refs):
    ups, downs = refs[:n_up], refs[n_up : n_up + n_down]
    outs, sems = refs[n_up + n_down : -1], refs[-1]
    for i in range(count):
        fetch(sched[0, first + i], per, own, ups, (), limit, outs[2 * i], sems.at[2 * i])
        fetch(sched[1, first + i], per, own, downs, (), limit, outs[2 * i + 1], sems.at[2 * i + 1])
    for i in range(2 * count):
        pltpu.make_async_copy(own.at[0], outs[i], sems.at[i]).wait()


def pick_sends(sched, own, ups, downs, first, count, limit):
    anywhere = pl.BlockSpec(memory_space=pl.ANY)
    one = jax.ShapeDtypeStruct(own.shape[1:], own.dtype)
    return pl.pallas_call(
        functools.partial(
            pick_kernel, first, count, own.shape[0], limit, len(ups), len(downs)
        ),
        out_shape=[one] * (2 * count),
        in_specs=[pl.BlockSpec(memory_space=SMEM)] + [anywhere] * (1 + len(ups) + len(downs)),
        out_specs=[anywhere] * (2 * count),
        scratch_shapes=[pltpu.SemaphoreType.DMA((2 * count,))],
        name="pick",
    )(sched, own, *ups, *downs)


def gather_kernel(per, limit, requests, n_up, n_down, sched, z, own, *refs):
    ups, downs = refs[:n_up], refs[n_up : n_up + n_down]
    out, sems = refs[-2], refs[-1]
    for r in range(requests):
        fetch(sched[2, z[0] * requests + r], per, own, ups, downs, limit, out.at[r], sems.at[r])
    for r in range(requests):
        pltpu.make_async_copy(own.at[0], out.at[r], sems.at[r]).wait()


def gather_own(sched, z, own, ups, downs, requests, limit):
    anywhere = pl.BlockSpec(memory_space=pl.ANY)
    return pl.pallas_call(
        functools.partial(gather_kernel, own.shape[0], limit, requests, len(ups), len(downs)),
        out_shape=jax.ShapeDtypeStruct((requests,) + own.shape[1:], own.dtype),
        in_specs=[pl.BlockSpec(memory_space=SMEM)] * 2 + [anywhere] * (1 + len(ups) + len(downs)),
        out_specs=anywhere,
        scratch_shapes=[pltpu.SemaphoreType.DMA((requests,))],
        name="gather_own",
    )(sched, z, own, *ups, *downs)


def later_rounds(sched, z, own, ups, downs, requests, limit, n_dp):
    up, down = line(n_dp)
    per = own.shape[0]
    made = len(ups)
    spare = jnp.zeros((limit - made,) + own.shape[1:], own.dtype)
    up_all = jnp.concatenate([jnp.stack(ups), spare])
    down_all = jnp.concatenate([jnp.stack(downs), spare])

    def choose(code, came):
        held = lax.dynamic_index_in_dim(own, jnp.minimum(code, per - 1), 0, keepdims=False)
        passed = lax.dynamic_index_in_dim(came, jnp.clip(code - per, 0, limit - 1), 0, keepdims=False)
        return jnp.where(code < per, held, passed)

    def step(carry):
        k, up_all, down_all = carry
        from_below = lax.ppermute(choose(sched[0, k], up_all), "dp", up)
        from_above = lax.ppermute(choose(sched[1, k], down_all), "dp", down)
        up_all = lax.dynamic_update_index_in_dim(up_all, from_below, k, 0)
        down_all = lax.dynamic_update_index_in_dim(down_all, from_above, k, 0)
        return k + 1, up_all, down_all

    _, up_all, down_all = lax.while_loop(
        lambda c: c[0] < sched[3, 0], step, (jnp.int32(made), up_all, down_all)
    )
    places = lax.dynamic_slice(sched, (2, z[0] * requests), (1, requests))[0]
    picked = []
    for r in range(requests):
        code = places[r]
        below = choose(code, up_all)
        above = lax.dynamic_index_in_dim(
            down_all, jnp.clip(code - per - limit, 0, limit - 1), 0, keepdims=False
        )
        picked.append(jnp.where(code >= per + limit, above, below))
    return jnp.stack(picked)


def line(n):
    return [(i, i + 1) for i in range(n - 1)], [(i + 1, i) for i in range(n - 1)]


def bring_adapters(sched, z, own, requests, n_dp):
    up, down = line(n_dp)
    limit = most_rounds(n_dp, requests)
    rounds = min(ROUNDS, limit)
    ups, downs = [], []
    ahead = []
    for k in range(rounds):
        if k < LAG:
            if k == 0:
                ahead = pick_sends(sched, own, [], [], 0, min(LAG, rounds), limit)
            sends = ahead[2 * k : 2 * k + 2]
        else:
            known = k - LAG + 1
            sends = pick_sends(sched, own, ups[:known], downs[:known], k, 1, limit)
        ups.append(lax.ppermute(sends[0], "dp", up))
        downs.append(lax.ppermute(sends[1], "dp", down))
    return lax.cond(
        sched[3, 0] > rounds,
        lambda: later_rounds(sched, z, own, ups, downs, requests, limit, n_dp),
        lambda: gather_own(sched, z, own, ups, downs, requests, limit),
    )


def by_core(n):
    return [(i, i ^ 1) for i in range(n)]


def by_chip(n):
    return [(i, i ^ 2) for i in range(n)]


def added(a, b):
    return (a.astype(F32) + b.astype(F32)).astype(BF16)


def all_sum(x, n_tensor):
    if n_tensor != 4:
        return lax.psum(x, "tensor")
    x = added(x, lax.ppermute(x, "tensor", by_core(n_tensor)))
    return added(x, lax.ppermute(x, "tensor", by_chip(n_tensor)))


def prefix_order(n):
    table = []
    for z in range(n):
        seen = []
        for hop in range(1, n):
            seen += [(hop, True)] if hop <= z else []
            seen += [(hop, False)] if hop <= n - 1 - z else []
        table.append(seen)
    return [[table[z][s] for z in range(n)] for s in range(n - 1)]


def per_device(
    n_groups,
    n_dp,
    n_tensor,
    queries,
    suffix_rotated_key_slots,
    suffix_value_slots,
    shared_prefix_key_slots,
    shared_prefix_value_slots,
    lengths,
    request_adapter_index,
    output_weight_matrix,
    adapter_down_factors,
    adapter_up_factors,
):
    tokens, width = queries.shape
    requests = lengths.shape[1]
    per = adapter_down_factors.shape[0]
    zi = lax.axis_index("dp").astype(jnp.int32)
    z = zi.reshape(1)
    ti = lax.axis_index("tensor").astype(jnp.int32)
    up, down = line(n_dp)

    lane = jnp.arange(128, dtype=jnp.int32) - zi * requests
    mine = jnp.zeros((128,), jnp.int32)
    for r in range(requests):
        mine = jnp.where(lane == r, request_adapter_index[0, r], mine)
    mine = mine[None]
    groups = [mine] + [
        lax.ppermute(mine, "groups", [(i, (i + s) % n_groups) for i in range(n_groups)])
        for s in range(1, n_groups)
    ]
    both = jnp.concatenate(groups, axis=0)
    known = both
    for s in range(1, n_dp):
        known = known + lax.ppermute(both, "dp", [(i, (i + s) % n_dp) for i in range(n_dp)])
    spare = [jnp.zeros((1, 128), jnp.int32)] * 4
    idx_rows = jnp.concatenate([known[0:1], known[0:1], known[1:2], known[1:2], *spare], axis=0)

    below = [(shared_prefix_key_slots, shared_prefix_value_slots)]
    above = [(shared_prefix_key_slots, shared_prefix_value_slots)]
    for hop in range(1, n_dp):
        below.append(tuple(lax.ppermute(a, "dp", up) for a in below[-1]))
        above.append(tuple(lax.ppermute(a, "dp", down) for a in above[-1]))

    position = jnp.arange(tokens, dtype=jnp.int32)
    seg_ends = jnp.cumsum(lengths[0])
    request_of = jnp.sum((position[:, None] >= seg_ends[None, :]).astype(jnp.int32), axis=1)
    seg_q = jnp.stack([request_of, position], axis=1)
    seg_k = request_of[None]

    keys = [suffix_rotated_key_slots, shared_prefix_key_slots]
    values = [suffix_value_slots, shared_prefix_value_slots]
    for choices in prefix_order(n_dp):
        pick = None
        for place, (hop, from_below) in enumerate(choices):
            arrived = below[hop] if from_below else above[hop]
            if pick is None:
                pick = arrived
            else:
                pick = tuple(jnp.where(zi == place, a, b) for a, b in zip(arrived, pick))
        keys.append(pick[0])
        values.append(pick[1])

    sched = make_schedule(n_dp, requests, per, idx_rows, z)
    down_rows = jnp.transpose(adapter_down_factors, (0, 2, 1))
    picked_down = bring_adapters(sched, z, down_rows, requests, n_dp)
    picked_up = bring_adapters(sched, z, adapter_up_factors, requests, n_dp)

    chunks = CHUNKS
    bases, attended = [], []
    for c in range(chunks):
        part = attend(queries, seg_q, seg_k, keys, values, c, chunks)
        attended.append(part)
        if n_tensor == 4:
            far_other, far_same, near_other, near_same = (
                project(part, output_weight_matrix, (ti ^ m).reshape(1), n_tensor)
                for m in (3, 2, 1, 0)
            )
            core, chip = by_core(n_tensor), by_chip(n_tensor)
            send = added(far_same, lax.ppermute(far_other, "tensor", core))
            arriving = lax.ppermute(send, "tensor", chip)
            near = near_same.astype(F32) + lax.ppermute(near_other, "tensor", core).astype(F32)
            bases.append(near + arriving.astype(F32))
        else:
            whole = project(part, output_weight_matrix, jnp.zeros((1,), jnp.int32), 1)
            share = lax.psum_scatter(whole, "tensor", scatter_dimension=1, tiled=True)
            bases.append(share.astype(F32))
    base = jnp.concatenate(bases, axis=0)
    attended = jnp.concatenate(attended, axis=0)

    select = request_of[:, None] == jnp.arange(requests, dtype=jnp.int32)[None, :]
    first = lax.dot_general(
        attended,
        picked_down.reshape(-1, width),
        (((1,), (1,)), ((), ())),
        preferred_element_type=F32,
    ).reshape(tokens, requests, -1)
    partial_shrink = jnp.sum(jnp.where(select[:, :, None], first, 0.0), axis=1).astype(BF16)
    shrink = all_sum(partial_shrink, n_tensor)
    spread = jnp.where(select[:, :, None], shrink[:, None, :], 0).reshape(tokens, -1)
    expand = jnp.dot(
        spread, picked_up.reshape(spread.shape[1], -1), preferred_element_type=F32
    )
    return (base + expand).astype(BF16)


def solution(mesh):
    return jax.shard_map(
        functools.partial(
            per_device, mesh.shape["groups"], mesh.shape["dp"], mesh.shape["tensor"]
        ),
        mesh=mesh,
        in_specs=(
            P(("groups", "dp"), "tensor"),
            P(("groups", "dp"), "tensor"),
            P(("groups", "dp"), "tensor"),
            P(("groups", "dp"), "tensor"),
            P(("groups", "dp"), "tensor"),
            P(("groups", "dp"), None),
            P(("groups", "dp"), None),
            P("tensor", None),
            P("dp", "tensor", None),
            P("dp", None, "tensor"),
        ),
        out_specs=P(("groups", "dp"), "tensor"),
        check_vma=False,
    )
```

```python
import functools
import math

import jax
import jax.numpy as jnp
from jax import lax
from jax.experimental import pallas as pl
from jax.experimental.pallas import tpu as pltpu
from jax.sharding import PartitionSpec as P

HD = 128
CAPS = (2, 2, 2, 1)
F32 = jnp.float32
BF16 = jnp.bfloat16
SMEM = pltpu.MemorySpace.SMEM
VMEM = pltpu.MemorySpace.VMEM


def params(mib=32, **more):
    return pltpu.CompilerParams(vmem_limit_bytes=mib * 1024 * 1024, **more)


def attend_kernel(order, scale, place, seg_q, seg_k, q_ref, key_ref, value_ref, own_ref, *refs):
    hops = len(order)
    below, above = refs[:hops], refs[hops : 2 * hops]
    out_ref, bias, ones_beside, held, sems = refs[2 * hops :]
    tokens, group = q_ref.shape[0], q_ref.shape[1] // HD
    rows = own_ref.shape[0]
    slots = own_ref.shape[1] // (2 * HD)
    slot = pl.program_id(0)

    @pl.when(slot == 0)
    def _():
        pltpu.make_async_copy(own_ref, held.at[0], sems.at[0]).start()
        for step, choices in enumerate(order):
            for hop, from_below in sorted(set(choices)):
                here = functools.reduce(
                    jnp.logical_or,
                    [place[0] == i for i, c in enumerate(choices) if c == (hop, from_below)],
                )

                @pl.when(here)
                def _(ref=(below if from_below else above)[hop - 1], to=step + 1):
                    pltpu.make_async_copy(ref, held.at[to], sems.at[to]).start()

        same = seg_q[:, 0:1] == seg_k[0:1, :]
        last = seg_q[:, 1:2]
        where_k = lax.broadcasted_iota(jnp.int32, bias.shape, 1)
        bias[...] = jnp.where(same & (where_k <= last), 0.0, -1e30)
        ones_beside[:, HD:] = jnp.ones((ones_beside.shape[0], HD), BF16)
        for i in range(hops + 1):
            pltpu.make_async_copy(own_ref, held.at[i], sems.at[i]).wait()

    key_at = pl.ds(pl.multiple_of(slot * HD, HD), HD)
    value_at = pl.ds(pl.multiple_of((slots + slot) * HD, HD), HD)
    ones_beside[:tokens, :HD] = value_ref[...]
    for i in range(hops + 1):
        ones_beside[tokens + i * rows : tokens + (i + 1) * rows, :HD] = held[i, :, value_at]
    dims = (((1,), (1,)), ((), ()))
    factor = scale * math.log2(math.e)
    for h in range(group):
        q = q_ref[:, h * HD : (h + 1) * HD]
        peak = None
        for i in range(hops + 2):
            keys = key_ref[...] if i == 0 else held[i - 1, :, key_at]
            s = lax.dot_general(q, keys, dims, preferred_element_type=F32)
            if i == 0:
                s = s + bias[...]
                at = slice(0, tokens)
            else:
                at = slice(tokens + (i - 1) * rows, tokens + i * rows)
            high = jnp.max(s, axis=1, keepdims=True)
            high = high if peak is None else jnp.maximum(peak, high)
            w = jnp.exp2((s - high) * factor)
            o = jnp.dot(w.astype(BF16), ones_beside[at, :], preferred_element_type=F32)
            summed = o if peak is None else summed * jnp.exp2((peak - high) * factor) + o
            peak = high
        out_ref[:, h * HD : (h + 1) * HD] = (summed[:, :HD] / summed[:, HD:]).astype(BF16)


def attend(z, q, seg_q, seg_k, keys, values, own, below, above):
    tokens, width = q.shape
    rows = own.shape[0]
    slots = own.shape[1] // (2 * HD)
    wide = width // slots
    order = prefix_order(len(below) + 1)
    n_keys = tokens + (len(below) + 1) * rows
    anywhere = pl.BlockSpec(memory_space=pl.ANY)
    return pl.pallas_call(
        functools.partial(attend_kernel, order, 1.0 / math.sqrt(HD)),
        grid=(slots,),
        out_shape=jax.ShapeDtypeStruct((tokens, width), BF16),
        in_specs=[
            pl.BlockSpec(memory_space=SMEM),
            pl.BlockSpec((tokens, 2), lambda s: (0, 0)),
            pl.BlockSpec((1, tokens), lambda s: (0, 0)),
            pl.BlockSpec((tokens, wide), lambda s: (0, s)),
            pl.BlockSpec((tokens, HD), lambda s: (0, s)),
            pl.BlockSpec((tokens, HD), lambda s: (0, s)),
            anywhere,
        ]
        + [anywhere] * (2 * len(below)),
        out_specs=pl.BlockSpec((tokens, wide), lambda s: (0, s)),
        scratch_shapes=[
            pltpu.VMEM((tokens, tokens), F32),
            pltpu.VMEM((n_keys, 2 * HD), BF16),
            pltpu.VMEM((len(below) + 1,) + own.shape, BF16),
            pltpu.SemaphoreType.DMA((len(below) + 1,)),
        ],
        compiler_params=params(44),
        cost_estimate=pl.CostEstimate(
            flops=8 * tokens * n_keys * width, bytes_accessed=4 * tokens * width, transcendentals=0
        ),
        name="attend",
    )(z, seg_q, seg_k, q, keys, values, own, *below, *above)


def project_kernel(which, a_ref, w_ref, out_ref):
    out_ref[...] = jnp.dot(a_ref[...], w_ref[...], preferred_element_type=F32).astype(BF16)


def project(a, w, block, count):
    rows, depth = a.shape
    wide = w.shape[1] // count
    tile = min(1024, wide)
    steps = wide // tile
    return pl.pallas_call(
        project_kernel,
        out_shape=jax.ShapeDtypeStruct((rows, wide), BF16),
        grid_spec=pltpu.PrefetchScalarGridSpec(
            num_scalar_prefetch=1,
            grid=(steps,),
            in_specs=[
                pl.BlockSpec((rows, depth), lambda j, which: (0, 0)),
                pl.BlockSpec((depth, tile), lambda j, which: (0, which[0] * steps + j)),
            ],
            out_specs=pl.BlockSpec((rows, tile), lambda j, which: (0, j)),
        ),
        compiler_params=params(32),
        cost_estimate=pl.CostEstimate(
            flops=2 * rows * depth * wide, bytes_accessed=2 * depth * wide, transcendentals=0
        ),
        name="project",
    )(block, a, w)


def most_slots(n_dp, requests):
    return sum(CAPS) + requests * (n_dp - 1) + n_dp


def schedule_kernel(n_dp, requests, per, idx_ref, z_ref, out_ref):
    limit = most_slots(n_dp, requests)
    links = n_dp - 1
    idx = idx_ref[...]
    shape = idx.shape
    z = z_ref[0]
    lane = lax.broadcasted_iota(jnp.int32, shape, 1)
    row = lax.broadcasted_iota(jnp.int32, shape, 0)
    link = lax.broadcasted_iota(jnp.int32, (links,) + shape, 0)
    valid = (lane < n_dp * requests) & (row < 4)
    down = (row % 2) == 1
    taker = lane // requests
    holder = idx // per
    local = idx % per
    own = valid & (taker == holder)
    dst = jnp.where(down, n_dp - 1 - taker, taker)
    src = jnp.where(down, n_dp - 1 - holder, holder)
    me = jnp.where(down, n_dp - 1 - z, z)
    moving = valid & (src < dst)
    dst = jnp.where(moving, dst, 0)
    pos = jnp.where(moving, src, 0)
    rank = dst * 256 + 255 - lane
    zero = jnp.zeros(shape, jnp.int32)

    def one_round(first, slots, pos, came, codes):
        can = (pos[None] == link) & (dst[None] > link)
        code = jnp.where(src == me, local, per + came)
        moved = zero
        for slot in range(slots):
            key = jnp.where(can, rank[None], -1)
            best = jnp.max(key, axis=2, keepdims=True)
            chosen = can & (key == best)
            can = can & ~chosen
            sent = jnp.sum(jnp.where(chosen & (link == me[None]), code[None], 0), axis=0)
            codes = jnp.where(lane == first + slot, jnp.sum(sent, axis=1, keepdims=True), codes)
            got = jnp.sum(jnp.where(chosen & (link + 1 == me[None]), 1, 0), axis=0)
            came = jnp.where(got > 0, first + slot, came)
            moved = moved + jnp.sum(jnp.where(chosen, 1, 0), axis=0)
        return pos + moved, came, codes

    came, codes = zero, zero
    first = 0
    for slots in CAPS:
        pos, came, codes = one_round(first, slots, pos, came, codes)
        first += slots

    def left(pos):
        return jnp.max(jnp.where(pos < dst, 1, 0))

    def later(carry):
        k, _, pos, came, codes = carry
        pos, came, codes = one_round(k, 1, pos, came, codes)
        return k + 1, left(pos), pos, came, codes

    used, _, _, came, codes = lax.while_loop(
        lambda c: (c[1] > 0) & (c[0] < limit), later, (jnp.int32(first), left(pos), pos, came, codes)
    )
    place = jnp.where(own & (row == 0), local, 0)
    place = place + jnp.where(moving & (row == 0), per + came, 0)
    place = place + jnp.where(moving & (row == 1), per + limit + came, 0)
    place = jnp.sum(jnp.where(row < 2, place, 0), axis=0, keepdims=True)
    out = jnp.where(row < 2, codes, 0)
    out = jnp.where(row == 2, place, out)
    out_ref[...] = jnp.where(row == 3, used, out)


def make_schedule(n_dp, requests, per, idx_rows, z):
    return pl.pallas_call(
        functools.partial(schedule_kernel, n_dp, requests, per),
        out_shape=jax.ShapeDtypeStruct((8, 128), jnp.int32),
        in_specs=[pl.BlockSpec(memory_space=VMEM), pl.BlockSpec(memory_space=SMEM)],
        out_specs=pl.BlockSpec(memory_space=VMEM),
        name="schedule",
    )(idx_rows, z)


def slots_of(came):
    return [(r, j) for r, ref in enumerate(came) for j in range(CAPS[r])]


def fetch(code, per, own, ups, downs, limit, out, sems):
    rank = own[0].shape[1]

    @pl.when(code < per)
    def _():
        at = jnp.minimum(code, per - 1)
        for half in range(2):
            to = out.at[half * rank : (half + 1) * rank]
            pltpu.make_async_copy(own[half].at[at], to, sems.at[half]).start()

    for base, came in ((per, ups), (per + limit, downs)):
        for k, (r, j) in enumerate(slots_of(came)):

            @pl.when(code == base + k)
            def _(ref=came[r], j=j):
                for half in range(2):
                    part = slice(half * rank, (half + 1) * rank)
                    pltpu.make_async_copy(ref.at[j, part], out.at[part], sems.at[half]).start()


def fetched(own, out, sems):
    rank = own[0].shape[1]
    for half in range(2):
        to = out.at[half * rank : (half + 1) * rank]
        pltpu.make_async_copy(own[half].at[0], to, sems.at[half]).wait()


def pick_kernel(first, count, per, limit, n_came, sched, down_ref, up_ref, *refs):
    ups, downs = refs[:n_came], refs[n_came : 2 * n_came]
    outs, sems = refs[2 * n_came : -1], refs[-1]
    own = (down_ref, up_ref)
    for i in range(count):
        for way, came in enumerate((ups, downs)):
            code = sched[way, first + i]
            fetch(code, per, own, came, (), limit, outs[way].at[i], sems.at[way, i])
    for i in range(count):
        for way in range(2):
            fetched(own, outs[way].at[i], sems.at[way, i])


def slot_shape(own):
    return (2 * own[0].shape[1], own[0].shape[2])


def pick_sends(sched, own, ups, downs, number, limit):
    count, first = CAPS[number], sum(CAPS[:number])
    anywhere = pl.BlockSpec(memory_space=pl.ANY)
    in_vmem = pl.BlockSpec(memory_space=VMEM)
    out = jax.ShapeDtypeStruct((count,) + slot_shape(own), BF16)
    return pl.pallas_call(
        functools.partial(pick_kernel, first, count, own[0].shape[0], limit, len(ups)),
        out_shape=[out] * 2,
        in_specs=[pl.BlockSpec(memory_space=SMEM)] + [anywhere] * (2 + 2 * len(ups)),
        out_specs=[in_vmem] * 2,
        scratch_shapes=[pltpu.SemaphoreType.DMA((2, count, 2))],
        compiler_params=params(16),
        name="pick",
    )(sched, *own, *ups, *downs)


def gather_kernel(per, limit, requests, n_came, sched, z, down_ref, up_ref, *refs):
    ups, downs = refs[:n_came], refs[n_came : 2 * n_came]
    out, sems = refs[-2], refs[-1]
    own = (down_ref, up_ref)
    for r in range(requests):
        code = sched[2, z[0] * requests + r]
        fetch(code, per, own, ups, downs, limit, out.at[r], sems.at[r])
    for r in range(requests):
        fetched(own, out.at[r], sems.at[r])


def gather_own(sched, z, own, ups, downs, requests, limit):
    anywhere = pl.BlockSpec(memory_space=pl.ANY)
    return pl.pallas_call(
        functools.partial(gather_kernel, own[0].shape[0], limit, requests, len(ups)),
        out_shape=jax.ShapeDtypeStruct((requests,) + slot_shape(own), BF16),
        in_specs=[pl.BlockSpec(memory_space=SMEM)] * 2 + [anywhere] * (2 + 2 * len(ups)),
        out_specs=pl.BlockSpec(memory_space=VMEM),
        scratch_shapes=[pltpu.SemaphoreType.DMA((requests, 2))],
        compiler_params=params(16),
        name="gather_own",
    )(sched, z, *own, *ups, *downs)


def later_rounds(sched, z, own, ups, downs, requests, limit, n_dp):
    up, down = line(n_dp)
    per = own[0].shape[0]
    made = sum(CAPS)
    spare = jnp.zeros((limit - made,) + slot_shape(own), BF16)
    up_all = jnp.concatenate([*ups, spare])
    down_all = jnp.concatenate([*downs, spare])

    def choose(code, came):
        at = jnp.minimum(code, per - 1)
        held = [lax.dynamic_index_in_dim(o, at, 0, keepdims=False) for o in own]
        passed = lax.dynamic_index_in_dim(came, jnp.clip(code - per, 0, limit - 1), 0, keepdims=False)
        return jnp.where(code < per, jnp.concatenate(held), passed)

    def step(carry):
        k, up_all, down_all = carry
        from_below = lax.ppermute(choose(sched[0, k], up_all), "dp", up)
        from_above = lax.ppermute(choose(sched[1, k], down_all), "dp", down)
        up_all = lax.dynamic_update_index_in_dim(up_all, from_below, k, 0)
        down_all = lax.dynamic_update_index_in_dim(down_all, from_above, k, 0)
        return k + 1, up_all, down_all

    _, up_all, down_all = lax.while_loop(
        lambda c: c[0] < sched[3, 0], step, (jnp.int32(made), up_all, down_all)
    )
    places = lax.dynamic_slice(sched, (2, z[0] * requests), (1, requests))[0]
    picked = []
    for r in range(requests):
        code = places[r]
        below = choose(code, up_all)
        above = lax.dynamic_index_in_dim(
            down_all, jnp.clip(code - per - limit, 0, limit - 1), 0, keepdims=False
        )
        picked.append(jnp.where(code >= per + limit, above, below))
    return jnp.stack(picked)


def line(n):
    return [(i, i + 1) for i in range(n - 1)], [(i + 1, i) for i in range(n - 1)]


def bring_adapters(sched, z, own, requests, n_dp):
    up, down = line(n_dp)
    limit = most_slots(n_dp, requests)
    ups, downs = [], []
    for number in range(len(CAPS)):
        sends = pick_sends(sched, own, ups, downs, number, limit)
        ups.append(lax.ppermute(sends[0], "dp", up))
        downs.append(lax.ppermute(sends[1], "dp", down))
    return lax.cond(
        sched[3, 0] > sum(CAPS),
        lambda: later_rounds(sched, z, own, ups, downs, requests, limit, n_dp),
        lambda: gather_own(sched, z, own, ups, downs, requests, limit),
    )


def by_core(n):
    return [(i, i ^ 1) for i in range(n)]


def by_chip(n):
    return [(i, i ^ 2) for i in range(n)]


def added(a, b):
    return (a.astype(F32) + b.astype(F32)).astype(BF16)


def all_sum(x, n_tensor):
    if n_tensor != 4:
        return lax.psum(x, "tensor")
    x = added(x, lax.ppermute(x, "tensor", by_core(n_tensor)))
    return added(x, lax.ppermute(x, "tensor", by_chip(n_tensor)))


def prefix_order(n):
    table = []
    for z in range(n):
        seen = []
        for hop in range(1, n):
            seen += [(hop, True)] if hop <= z else []
            seen += [(hop, False)] if hop <= n - 1 - z else []
        table.append(seen)
    return [[table[z][s] for z in range(n)] for s in range(n - 1)]


def per_device(
    n_groups,
    n_dp,
    n_tensor,
    queries,
    suffix_rotated_key_slots,
    suffix_value_slots,
    shared_prefix_key_slots,
    shared_prefix_value_slots,
    lengths,
    request_adapter_index,
    output_weight_matrix,
    adapter_down_factors,
    adapter_up_factors,
):
    tokens, width = queries.shape
    requests = lengths.shape[1]
    per = adapter_down_factors.shape[0]
    zi = lax.axis_index("dp").astype(jnp.int32)
    z = zi.reshape(1)
    ti = lax.axis_index("tensor").astype(jnp.int32)
    up, down = line(n_dp)

    everyone = lax.all_gather(request_adapter_index, ("groups", "dp"), axis=0, tiled=True)
    everyone = jnp.pad(everyone.reshape(n_groups, -1), ((0, 0), (0, 128 - n_dp * requests)))
    gi = lax.axis_index("groups")
    mine = lax.dynamic_index_in_dim(everyone, gi, 0)
    other = lax.dynamic_index_in_dim(everyone, (gi + 1) % n_groups, 0)
    idx_rows = jnp.concatenate([mine, mine, other, other, jnp.zeros((4, 128), jnp.int32)], axis=0)

    own_rows = jnp.concatenate([shared_prefix_key_slots, shared_prefix_value_slots], axis=1)
    below, above = [own_rows], [own_rows]
    for hop in range(1, n_dp):
        below.append(lax.ppermute(below[-1], "dp", up[hop - 1 :]))
        above.append(lax.ppermute(above[-1], "dp", down[: n_dp - hop]))

    position = jnp.arange(tokens, dtype=jnp.int32)
    seg_ends = jnp.cumsum(lengths[0])
    request_of = jnp.sum((position[:, None] >= seg_ends[None, :]).astype(jnp.int32), axis=1)
    seg_q = jnp.stack([request_of, position], axis=1)
    seg_k = request_of[None]

    down_rows = jnp.transpose(adapter_down_factors, (0, 2, 1))
    idx_rows, _ = lax.optimization_barrier((idx_rows, (below[1], above[1])))
    sched = make_schedule(n_dp, requests, per, idx_rows, z)
    picked = bring_adapters(sched, z, (down_rows, adapter_up_factors), requests, n_dp)
    rank = picked.shape[1] // 2
    picked_down, picked_up = picked[:, :rank], picked[:, rank:]

    attended = attend(
        z,
        queries,
        seg_q,
        seg_k,
        suffix_rotated_key_slots,
        suffix_value_slots,
        own_rows,
        below[1:],
        above[1:],
    )
    if n_tensor == 4:
        far_other, far_same, near_other, near_same = (
            project(attended, output_weight_matrix, (ti ^ m).reshape(1), n_tensor)
            for m in (3, 2, 1, 0)
        )
        core, chip = by_core(n_tensor), by_chip(n_tensor)
        send = added(far_same, lax.ppermute(far_other, "tensor", core))
        arriving = lax.ppermute(send, "tensor", chip)
        near = near_same.astype(F32) + lax.ppermute(near_other, "tensor", core).astype(F32)
        base = near + arriving.astype(F32)
    else:
        whole = project(attended, output_weight_matrix, jnp.zeros((1,), jnp.int32), 1)
        share = lax.psum_scatter(whole, "tensor", scatter_dimension=1, tiled=True)
        base = share.astype(F32)

    select = request_of[:, None] == jnp.arange(requests, dtype=jnp.int32)[None, :]
    first = lax.dot_general(
        attended,
        picked_down.reshape(-1, width),
        (((1,), (1,)), ((), ())),
        preferred_element_type=F32,
    ).reshape(tokens, requests, -1)
    partial_shrink = jnp.sum(jnp.where(select[:, :, None], first, 0.0), axis=1).astype(BF16)
    shrink = all_sum(partial_shrink, n_tensor)
    spread = jnp.where(select[:, :, None], shrink[:, None, :], 0).reshape(tokens, -1)
    expand = jnp.dot(
        spread, picked_up.reshape(spread.shape[1], -1), preferred_element_type=F32
    )
    return (base + expand).astype(BF16)


def solution(mesh):
    return jax.shard_map(
        functools.partial(
            per_device, mesh.shape["groups"], mesh.shape["dp"], mesh.shape["tensor"]
        ),
        mesh=mesh,
        in_specs=(
            P(("groups", "dp"), "tensor"),
            P(("groups", "dp"), "tensor"),
            P(("groups", "dp"), "tensor"),
            P(("groups", "dp"), "tensor"),
            P(("groups", "dp"), "tensor"),
            P(("groups", "dp"), None),
            P(("groups", "dp"), None),
            P("tensor", None),
            P("dp", "tensor", None),
            P("dp", None, "tensor"),
        ),
        out_specs=P(("groups", "dp"), "tensor"),
        check_vma=False,
    )
```

```python
import functools
import math

import jax
import jax.numpy as jnp
from jax import lax
from jax.experimental import pallas as pl
from jax.experimental.pallas import tpu as pltpu
from jax.sharding import PartitionSpec as P

HD = 128
CAPS = (2, 2, 2, 1)
PIECES = 4
SMALL = pl.CostEstimate(flops=1, bytes_accessed=1, transcendentals=0)
F32 = jnp.float32
BF16 = jnp.bfloat16
SMEM = pltpu.MemorySpace.SMEM
VMEM = pltpu.MemorySpace.VMEM


def cost(flops):
    return pl.CostEstimate(flops=flops, bytes_accessed=1, transcendentals=0)


def params(mib=32, **more):
    return pltpu.CompilerParams(vmem_limit_bytes=mib * 1024 * 1024, **more)


def attend_block(q, keys, values, bias, factor, peak, summed):
    s = lax.dot_general(q, keys, (((1,), (1,)), ((), ())), preferred_element_type=F32)
    if bias is not None:
        s = s + bias
    high = jnp.max(s, axis=1, keepdims=True)
    high = high if peak is None else jnp.maximum(peak, high)
    w = jnp.exp2((s - high) * factor)
    o = jnp.dot(w.astype(BF16), values, preferred_element_type=F32)
    if peak is not None:
        o = summed * jnp.exp2((peak - high) * factor) + o
    return high, o


def near_kernel(factor, seg_q, seg_k, q_ref, sk_ref, sv_ref, pk_ref, pv_ref, out_ref, stat_ref, bias, both):
    tokens, group = q_ref.shape[0], q_ref.shape[1] // HD

    @pl.when(pl.program_id(0) == 0)
    def _():
        same = seg_q[:, 0:1] == seg_k[0:1, :]
        last = seg_q[:, 1:2]
        where_k = lax.broadcasted_iota(jnp.int32, bias.shape, 1)
        bias[...] = jnp.where(same & (where_k <= last), 0.0, -1e30)
        both[:, HD:] = jnp.ones((both.shape[0], HD), BF16)
        both[:tokens, :HD] = sv_ref[...]
        both[tokens:, :HD] = pv_ref[...]

    for h in range(group):
        q = q_ref[:, h * HD : (h + 1) * HD]
        peak, summed = attend_block(q, sk_ref[...], both[:tokens], bias[...], factor, None, None)
        peak, summed = attend_block(q, pk_ref[...], both[tokens:], None, factor, peak, summed)
        at = slice(h * HD, (h + 1) * HD)
        out_ref[:, at] = summed[:, :HD] / summed[:, HD:]
        stat_ref[:, at] = peak * factor + jnp.log2(summed[:, HD:])


def far_kernel(order, factor, slot, slots, place, q_ref, near_ref, stat_ref, *refs):
    hops = len(order)
    below, above = refs[:hops], refs[hops : 2 * hops]
    out_ref, keys, both, held, sems = refs[2 * hops :]
    group = q_ref.shape[1] // HD
    rows = held.shape[1]
    @pl.when(pl.program_id(0) == 0)
    def _():
        for step, choices in enumerate(order):
            for hop, from_below in sorted(set(choices)):
                here = functools.reduce(
                    jnp.logical_or,
                    [place[0] == i for i, c in enumerate(choices) if c == (hop, from_below)],
                )

                @pl.when(here)
                def _(ref=(below if from_below else above)[hop - 1], to=step):
                    pltpu.make_async_copy(ref, held.at[to], sems.at[to]).start()

        both[:, HD:] = jnp.ones((both.shape[0], HD), BF16)
        for i in range(hops):
            pltpu.make_async_copy(below[0], held.at[i], sems.at[i]).wait()
            keys[i * rows : (i + 1) * rows] = held[i, :, slot * HD : (slot + 1) * HD]
            both[i * rows : (i + 1) * rows, :HD] = held[i, :, (slots + slot) * HD : (slots + slot + 1) * HD]

    for h in range(group):
        at = slice(h * HD, (h + 1) * HD)
        q = q_ref[:, at]
        peak, summed = None, None
        for i in range(hops):
            block = slice(i * rows, (i + 1) * rows)
            peak, summed = attend_block(q, keys[block], both[block], None, factor, peak, summed)
        far, near = jnp.broadcast_to(peak * factor, q.shape), stat_ref[:, at]
        high = jnp.maximum(far, near)
        far, near = jnp.exp2(far - high), jnp.exp2(near - high)
        result = summed[:, :HD] * far + near_ref[:, at] * near
        out_ref[:, at] = (result / (summed[:, HD:] * far + near)).astype(BF16)


FACTOR = math.log2(math.e) / math.sqrt(HD)


def attend_near(slot, q, seg_q, seg_k, keys, values, prefix_keys, prefix_values):
    tokens, width = q.shape
    rows, slots = prefix_keys.shape[0], prefix_keys.shape[1] // HD
    wide = width // slots
    halves = 2 if (wide // HD) % 2 == 0 else 1
    one = lambda n: pl.BlockSpec((n, HD), lambda s: (0, slot))
    out = pl.BlockSpec((tokens, wide // halves), lambda s: (0, s))
    return pl.pallas_call(
        functools.partial(near_kernel, FACTOR),
        grid=(halves,),
        out_shape=[jax.ShapeDtypeStruct((tokens, wide), F32)] * 2,
        in_specs=[
            pl.BlockSpec((tokens, 2), lambda s: (0, 0)),
            pl.BlockSpec((1, tokens), lambda s: (0, 0)),
            pl.BlockSpec((tokens, wide // halves), lambda s: (0, slot * halves + s)),
            one(tokens),
            one(tokens),
            one(rows),
            one(rows),
        ],
        out_specs=[out] * 2,
        scratch_shapes=[
            pltpu.VMEM((tokens, tokens), F32),
            pltpu.VMEM((tokens + rows, 2 * HD), BF16),
        ],
        compiler_params=params(58),
        cost_estimate=cost(16 * tokens * (tokens + rows) * wide),
        name="attend_near",
    )(seg_q, seg_k, q, keys, values, prefix_keys, prefix_values)


def attend_far(slot, slots, z, q, near, stats, below, above):
    tokens, wide = near.shape
    rows, hops = below[0].shape[0], len(below)
    halves = 2 if (wide // HD) % 2 == 0 else 1
    one = pl.BlockSpec((tokens, wide // halves), lambda s: (0, s))
    anywhere = pl.BlockSpec(memory_space=pl.ANY)
    return pl.pallas_call(
        functools.partial(far_kernel, prefix_order(hops + 1), FACTOR, slot, slots),
        grid=(halves,),
        out_shape=jax.ShapeDtypeStruct((tokens, wide), BF16),
        in_specs=[
            pl.BlockSpec(memory_space=SMEM),
            pl.BlockSpec((tokens, wide // halves), lambda s: (0, slot * halves + s)),
            one,
            one,
        ]
        + [anywhere] * (2 * hops),
        out_specs=one,
        scratch_shapes=[
            pltpu.VMEM((hops * rows, HD), BF16),
            pltpu.VMEM((hops * rows, 2 * HD), BF16),
            pltpu.VMEM((hops,) + below[0].shape, BF16),
            pltpu.SemaphoreType.DMA((hops,)),
        ],
        compiler_params=params(58),
        cost_estimate=cost(16 * tokens * hops * rows * wide),
        name="attend_far",
    )(z, q, near, stats, *below, *above)


def project_kernel(steps, n_parts, which, *refs):
    a_refs, w_ref, out_refs = refs[:n_parts], refs[n_parts], refs[n_parts + 1 :]
    part = a_refs[0].shape[1]
    result = sum(
        jnp.dot(a[...], w_ref[i * part : (i + 1) * part], preferred_element_type=F32)
        for i, a in enumerate(a_refs)
    ).astype(BF16)
    for i, out_ref in enumerate(out_refs):

        @pl.when(pl.program_id(0) // steps == i)
        def _(out_ref=out_ref):
            out_ref[...] = result


def project(parts, w, blocks, count, weigh=0):
    rows, depth = parts[0].shape[0], w.shape[0]
    wide = w.shape[1] // count
    tile = min(1024, wide)
    steps = wide // tile
    n = blocks.shape[0]

    def out_at(i):
        return lambda j, which: (0, jnp.clip(j - i * steps, 0, steps - 1))

    return pl.pallas_call(
        functools.partial(project_kernel, steps, len(parts)),
        out_shape=[jax.ShapeDtypeStruct((rows, wide), BF16)] * n,
        grid_spec=pltpu.PrefetchScalarGridSpec(
            num_scalar_prefetch=1,
            grid=(n * steps,),
            in_specs=[
                *[pl.BlockSpec(a.shape, lambda j, which: (0, 0)) for a in parts],
                pl.BlockSpec((depth, tile), lambda j, which: (0, which[j // steps] * steps + j % steps)),
            ],
            out_specs=[pl.BlockSpec((rows, tile), out_at(i)) for i in range(n)],
        ),
        compiler_params=params(58),
        cost_estimate=cost(1 + weigh * n * rows * depth * wide // 2),
        name="project",
    )(blocks, *parts, w)


def most_slots(n_dp, requests):
    return sum(CAPS) + requests * (n_dp - 1) + n_dp


def schedule_kernel(n_dp, requests, per, idx_ref, z_ref, out_ref):
    limit = most_slots(n_dp, requests)
    links = n_dp - 1
    idx = idx_ref[...]
    shape = idx.shape
    z = z_ref[0]
    lane = lax.broadcasted_iota(jnp.int32, shape, 1)
    row = lax.broadcasted_iota(jnp.int32, shape, 0)
    link = lax.broadcasted_iota(jnp.int32, (links,) + shape, 0)
    valid = (lane < n_dp * requests) & (row < 4)
    down = (row % 2) == 1
    taker = (z + n_dp - lane // requests) % n_dp
    holder = idx // per
    local = idx % per
    own = valid & (taker == holder)
    dst = jnp.where(down, n_dp - 1 - taker, taker)
    src = jnp.where(down, n_dp - 1 - holder, holder)
    me = jnp.where(down, n_dp - 1 - z, z)
    moving = valid & (src < dst)
    dst = jnp.where(moving, dst, 0)
    pos = jnp.where(moving, src, 0)
    rank = dst * 256 + 255 - (taker * requests + lane % requests)
    zero = jnp.zeros(shape, jnp.int32)

    def one_round(first, slots, pos, came, codes):
        can = (pos[None] == link) & (dst[None] > link)
        code = jnp.where(src == me, local, per + came)
        moved = zero
        for slot in range(slots):
            key = jnp.where(can, rank[None], -1)
            best = jnp.max(key, axis=2, keepdims=True)
            chosen = can & (key == best)
            can = can & ~chosen
            sent = jnp.sum(jnp.where(chosen & (link == me[None]), code[None], 0), axis=0)
            codes = jnp.where(lane == first + slot, jnp.sum(sent, axis=1, keepdims=True), codes)
            got = jnp.sum(jnp.where(chosen & (link + 1 == me[None]), 1, 0), axis=0)
            came = jnp.where(got > 0, first + slot, came)
            moved = moved + jnp.sum(jnp.where(chosen, 1, 0), axis=0)
        return pos + moved, came, codes

    came, codes = zero, zero
    first = 0

    def left(pos):
        return jnp.max(jnp.where(pos < dst, 1, 0))

    unfinished = []
    for slots in CAPS:
        unfinished.append(left(pos))
        pos, came, codes = one_round(first, slots, pos, came, codes)
        first += slots

    def later(carry):
        k, _, pos, came, codes = carry
        pos, came, codes = one_round(k, 1, pos, came, codes)
        return k + 1, left(pos), pos, came, codes

    used, _, _, came, codes = lax.while_loop(
        lambda c: (c[1] > 0) & (c[0] < limit), later, (jnp.int32(first), left(pos), pos, came, codes)
    )
    used = jnp.where(unfinished[-1] > 0, used, first - CAPS[-1])
    place = jnp.where(own & (row == 0), local, 0)
    place = place + jnp.where(moving & (row == 0), per + came, 0)
    place = place + jnp.where(moving & (row == 1), per + limit + came, 0)
    place = jnp.sum(jnp.where(row < 2, place, 0), axis=0, keepdims=True)
    out = jnp.where(row < 2, codes, 0)
    out = jnp.where(row == 2, place, out)
    out_ref[...] = jnp.where(row == 3, used, out)


def make_schedule(n_dp, requests, per, idx_rows, z):
    return pl.pallas_call(
        functools.partial(schedule_kernel, n_dp, requests, per),
        out_shape=jax.ShapeDtypeStruct((8, 128), jnp.int32),
        in_specs=[pl.BlockSpec(memory_space=VMEM), pl.BlockSpec(memory_space=SMEM)],
        out_specs=pl.BlockSpec(memory_space=VMEM),
        cost_estimate=SMALL,
        name="schedule",
    )(idx_rows, z)


def slots_of(came):
    return [(r, j) for r, ref in enumerate(came) for j in range(CAPS[r])]


def fetch(code, per, own, ups, downs, limit, out, sems):
    rank = own[0].shape[1]

    @pl.when(code < per)
    def _():
        at = jnp.minimum(code, per - 1)
        for half in range(2):
            to = out.at[half * rank : (half + 1) * rank]
            pltpu.make_async_copy(own[half].at[at], to, sems.at[half]).start()

    for base, came in ((per, ups), (per + limit, downs)):
        for k, (r, j) in enumerate(slots_of(came)):

            @pl.when(code == base + k)
            def _(ref=came[r], j=j):
                for half in range(2):
                    part = slice(half * rank, (half + 1) * rank)
                    pltpu.make_async_copy(ref.at[j, part], out.at[part], sems.at[half]).start()


def fetched(own, out, sems):
    rank = own[0].shape[1]
    for half in range(2):
        to = out.at[half * rank : (half + 1) * rank]
        pltpu.make_async_copy(own[half].at[0], to, sems.at[half]).wait()


def pick_kernel(first, count, per, limit, n_came, sched, down_ref, up_ref, *refs):
    ups, downs = refs[:n_came], refs[n_came : 2 * n_came]
    outs, sems = refs[2 * n_came : -1], refs[-1]
    own = (down_ref, up_ref)
    for i in range(count):
        for way, came in enumerate((ups, downs)):
            code = sched[way, first + i]
            fetch(code, per, own, came, (), limit, outs[way].at[i], sems.at[way, i])
    for i in range(count):
        for way in range(2):
            fetched(own, outs[way].at[i], sems.at[way, i])


def slot_shape(own):
    return (2 * own[0].shape[1], own[0].shape[2])


def pick_sends(sched, own, ups, downs, number, limit):
    count, first = CAPS[number], sum(CAPS[:number])
    anywhere = pl.BlockSpec(memory_space=pl.ANY)
    in_vmem = pl.BlockSpec(memory_space=VMEM)
    out = jax.ShapeDtypeStruct((count,) + slot_shape(own), BF16)
    return pl.pallas_call(
        functools.partial(pick_kernel, first, count, own[0].shape[0], limit, len(ups)),
        out_shape=[out] * 2,
        in_specs=[pl.BlockSpec(memory_space=SMEM)] + [anywhere] * (2 + 2 * len(ups)),
        out_specs=[in_vmem] * 2,
        scratch_shapes=[pltpu.SemaphoreType.DMA((2, count, 2))],
        compiler_params=params(16),
        cost_estimate=SMALL,
        name="pick",
    )(sched, *own, *ups, *downs)


def gather_kernel(per, limit, requests, n_came, sched, z, down_ref, up_ref, *refs):
    ups, downs = refs[:n_came], refs[n_came : 2 * n_came]
    out, sems = refs[-2], refs[-1]
    own = (down_ref, up_ref)
    for r in range(requests):
        code = sched[2, r]
        fetch(code, per, own, ups, downs, limit, out.at[r], sems.at[r])
    for r in range(requests):
        fetched(own, out.at[r], sems.at[r])


def gather_own(sched, z, own, ups, downs, requests, limit):
    anywhere = pl.BlockSpec(memory_space=pl.ANY)
    return pl.pallas_call(
        functools.partial(gather_kernel, own[0].shape[0], limit, requests, len(ups)),
        out_shape=jax.ShapeDtypeStruct((requests,) + slot_shape(own), BF16),
        in_specs=[pl.BlockSpec(memory_space=SMEM)] * 2 + [anywhere] * (2 + 2 * len(ups)),
        out_specs=pl.BlockSpec(memory_space=VMEM),
        scratch_shapes=[pltpu.SemaphoreType.DMA((requests, 2))],
        compiler_params=params(16),
        cost_estimate=SMALL,
        name="gather_own",
    )(sched, z, *own, *ups, *downs)


def later_rounds(sched, z, own, ups, downs, requests, limit, n_dp):
    up, down = line(n_dp)
    per = own[0].shape[0]
    made = sum(CAPS)
    spare = jnp.zeros((limit - made,) + slot_shape(own), BF16)
    up_all = jnp.concatenate([*ups, spare])
    down_all = jnp.concatenate([*downs, spare])

    def choose(code, came):
        at = jnp.minimum(code, per - 1)
        held = [lax.dynamic_index_in_dim(o, at, 0, keepdims=False) for o in own]
        passed = lax.dynamic_index_in_dim(came, jnp.clip(code - per, 0, limit - 1), 0, keepdims=False)
        return jnp.where(code < per, jnp.concatenate(held), passed)

    def step(carry):
        k, up_all, down_all = carry
        from_below = lax.ppermute(choose(sched[0, k], up_all), "dp", up)
        from_above = lax.ppermute(choose(sched[1, k], down_all), "dp", down)
        up_all = lax.dynamic_update_index_in_dim(up_all, from_below, k, 0)
        down_all = lax.dynamic_update_index_in_dim(down_all, from_above, k, 0)
        return k + 1, up_all, down_all

    _, up_all, down_all = lax.while_loop(
        lambda c: c[0] < sched[3, 0], step, (jnp.int32(made), up_all, down_all)
    )
    places = sched[2]
    picked = []
    for r in range(requests):
        code = places[r]
        below = choose(code, up_all)
        above = lax.dynamic_index_in_dim(
            down_all, jnp.clip(code - per - limit, 0, limit - 1), 0, keepdims=False
        )
        picked.append(jnp.where(code >= per + limit, above, below))
    return jnp.stack(picked)


def line(n):
    return [(i, i + 1) for i in range(n - 1)], [(i + 1, i) for i in range(n - 1)]


def adapter_round(sched, own, ups, downs, requests, n_dp, after=None):
    up, down = line(n_dp)
    sends = pick_sends(sched, own, ups, downs, len(ups), most_slots(n_dp, requests))
    sends, after = lax.optimization_barrier((sends, after))
    ups = ups + [lax.ppermute(sends[0], "dp", up)]
    downs = downs + [lax.ppermute(sends[1], "dp", down)]
    return ups, downs, after


def last_adapters(sched, z, own, ups, downs, requests, n_dp):
    limit = most_slots(n_dp, requests)

    def one_round():
        return adapter_round(sched, own, ups, downs, requests, n_dp)[:2]

    def enough():
        return gather_own(sched, z, own, ups, downs, requests, limit)

    def one_more():
        return gather_own(sched, z, own, *one_round(), requests, limit)

    def many_more():
        return later_rounds(sched, z, own, *one_round(), requests, limit, n_dp)

    used = sched[3, 0]
    short = (used > sum(CAPS[:-1])).astype(jnp.int32) + (used > sum(CAPS)).astype(jnp.int32)
    return lax.switch(short, (enough, one_more, many_more))


def by_core(n):
    return [(i, i ^ 1) for i in range(n)]


def by_chip(n):
    return [(i, i ^ 2) for i in range(n)]


def added(a, b):
    return (a.astype(F32) + b.astype(F32)).astype(BF16)


def all_sum(x, n_tensor):
    if n_tensor != 4:
        return lax.psum(x, "tensor")
    x = added(x, lax.ppermute(x, "tensor", by_core(n_tensor)))
    return added(x, lax.ppermute(x, "tensor", by_chip(n_tensor)))


def prefix_order(n):
    table = []
    for z in range(n):
        seen = []
        for hop in range(1, n):
            seen += [(hop, True)] if hop <= z else []
            seen += [(hop, False)] if hop <= n - 1 - z else []
        table.append(seen)
    return [[table[z][s] for z in range(n)] for s in range(n - 1)]


def per_device(
    n_groups,
    n_dp,
    n_tensor,
    queries,
    suffix_rotated_key_slots,
    suffix_value_slots,
    shared_prefix_key_slots,
    shared_prefix_value_slots,
    lengths,
    request_adapter_index,
    output_weight_matrix,
    adapter_down_factors,
    adapter_up_factors,
):
    tokens, width = queries.shape
    requests = lengths.shape[1]
    per = adapter_down_factors.shape[0]
    zi = lax.axis_index("dp").astype(jnp.int32)
    z = zi.reshape(1)
    ti = lax.axis_index("tensor").astype(jnp.int32)
    up, down = line(n_dp)

    own_rows = jnp.concatenate([shared_prefix_key_slots, shared_prefix_value_slots], axis=1)
    below, above = [own_rows], [own_rows]
    hop_first = (lax.ppermute(own_rows, "dp", up), lax.ppermute(own_rows, "dp", down))

    known = jnp.concatenate(
        [request_adapter_index]
        + [
            lax.ppermute(request_adapter_index, "dp", [(i, (i + s) % n_dp) for i in range(n_dp)])
            for s in range(1, n_dp)
        ],
        axis=1,
    )

    position = jnp.arange(tokens, dtype=jnp.int32)
    seg_ends = jnp.cumsum(lengths[0])
    request_of = jnp.sum((position[:, None] >= seg_ends[None, :]).astype(jnp.int32), axis=1)
    seg_q = jnp.stack([request_of, position], axis=1)
    seg_k = request_of[None]
    slots = shared_prefix_key_slots.shape[1] // HD

    def near_part(slot, q):
        return attend_near(
            slot,
            q,
            seg_q,
            seg_k,
            suffix_rotated_key_slots,
            suffix_value_slots,
            shared_prefix_key_slots,
            shared_prefix_value_slots,
        )

    nears = [near_part(0, queries)]
    hop_first, nears, known = lax.optimization_barrier((hop_first, nears, known))
    queries_here, hop_first = lax.optimization_barrier((queries, hop_first))
    nears += [near_part(slot, queries_here) for slot in range(1, slots)]
    for hop in range(1, n_dp):
        if hop == 1:
            from_below, from_above = hop_first
        else:
            from_below, from_above = below[-1], above[-1]
            if hop == 3:
                from_below, from_above, nears = lax.optimization_barrier(
                    (from_below, from_above, nears)
                )
            from_below = lax.ppermute(from_below, "dp", up[hop - 1 :])
            from_above = lax.ppermute(from_above, "dp", down[: n_dp - hop])
        below.append(from_below)
        above.append(from_above)

    own = (jnp.transpose(adapter_down_factors, (0, 2, 1)), adapter_up_factors)
    other = lax.ppermute(known, "groups", [(i, (i + 1) % n_groups) for i in range(n_groups)])
    rows = jnp.concatenate([known, known, other, other], axis=0)
    idx_rows = jnp.pad(rows, ((0, 8 - rows.shape[0]), (0, 128 - rows.shape[1])))
    sched = make_schedule(n_dp, requests, per, idx_rows, z)
    if n_dp > 2:
        sched, below[2], above[2] = lax.optimization_barrier((sched, below[2], above[2]))
    ups, downs, nears = adapter_round(sched, own, [], [], requests, n_dp, nears)
    attended = [
        attend_far(slot, slots, z, queries, *nears[slot], below[1:], above[1:])
        for slot in range(slots)
    ]
    ups, downs, attended = adapter_round(sched, own, ups, downs, requests, n_dp, attended)
    if n_tensor == 4:
        core, chip = by_core(n_tensor), by_chip(n_tensor)

        def share(parts, owners, weigh=0):
            pieces = jnp.arange(PIECES, dtype=jnp.int32)
            blocks = jnp.concatenate([owner * PIECES + pieces for owner in owners])
            return project(parts, output_weight_matrix, blocks, n_tensor * PIECES, weigh)

        far = share(attended, (ti ^ 3, ti ^ 2), 8)
        far_other, far_same = far[:PIECES], far[PIECES:]
        far_other, ups, downs = lax.optimization_barrier((far_other, ups, downs))
        from_core = [lax.ppermute(x, "tensor", core) for x in far_other]
        sends = [added(mine, came) for mine, came in zip(far_same, from_core)]
        sched, sends = lax.optimization_barrier((sched, sends))
        arriving = [lax.ppermute(x, "tensor", chip) for x in sends]
    ups, downs, again = adapter_round(sched, own, ups, downs, requests, n_dp, attended)
    if n_tensor == 4:
        near = share(again, (ti ^ 1, ti), 4)
        near_other, near_same = near[:PIECES], near[PIECES:]
        near_from_core = [lax.ppermute(x, "tensor", core) for x in near_other]
        sched, arriving[:2] = lax.optimization_barrier((sched, arriving[:2]))
    picked = last_adapters(sched, z, own, ups, downs, requests, n_dp)
    if n_tensor == 4:
        picked, arriving[2:-1] = lax.optimization_barrier((picked, arriving[2:-1]))
    rank = picked.shape[1] // 2
    picked_down, picked_up = picked[:, :rank], picked[:, rank:]
    select = request_of[:, None] == jnp.arange(requests, dtype=jnp.int32)[None, :]
    first = lax.dot_general(
        jnp.concatenate(attended, axis=1),
        picked_down.reshape(-1, width),
        (((1,), (1,)), ((), ())),
        preferred_element_type=F32,
    ).reshape(tokens, requests, -1)
    partial_shrink = jnp.sum(jnp.where(select[:, :, None], first, 0.0), axis=1).astype(BF16)
    if n_tensor == 4:
        bases = [
            mine.astype(F32) + near.astype(F32) + far.astype(F32)
            for mine, near, far in zip(near_same, near_from_core, arriving)
        ]
        base = jnp.concatenate(bases, axis=1)
    else:
        (whole,) = project(attended, output_weight_matrix, jnp.zeros((1,), jnp.int32), 1)
        share = lax.psum_scatter(whole, "tensor", scatter_dimension=1, tiled=True)
        base = share.astype(F32)
    shrink = all_sum(partial_shrink, n_tensor)
    spread = jnp.where(select[:, :, None], shrink[:, None, :], 0).reshape(tokens, -1)
    expand = jnp.dot(
        spread, picked_up.reshape(spread.shape[1], -1), preferred_element_type=F32
    )
    return (base + expand).astype(BF16)


def solution(mesh):
    return jax.shard_map(
        functools.partial(
            per_device, mesh.shape["groups"], mesh.shape["dp"], mesh.shape["tensor"]
        ),
        mesh=mesh,
        in_specs=(
            P(("groups", "dp"), "tensor"),
            P(("groups", "dp"), "tensor"),
            P(("groups", "dp"), "tensor"),
            P(("groups", "dp"), "tensor"),
            P(("groups", "dp"), "tensor"),
            P(("groups", "dp"), None),
            P(("groups", "dp"), None),
            P("tensor", None),
            P("dp", "tensor", None),
            P("dp", None, "tensor"),
        ),
        out_specs=P(("groups", "dp"), "tensor"),
        check_vma=False,
    )
```

```python
import functools
import math

import jax
import jax.numpy as jnp
from jax import lax
from jax.experimental import pallas as pl
from jax.experimental.pallas import tpu as pltpu
from jax.sharding import PartitionSpec as P

HD = 128
CAPS = (2, 2, 2, 1)
PIECES = 4
SMALL = pl.CostEstimate(flops=1, bytes_accessed=1, transcendentals=0)
F32 = jnp.float32
BF16 = jnp.bfloat16
SMEM = pltpu.MemorySpace.SMEM
VMEM = pltpu.MemorySpace.VMEM


def cost(flops):
    return pl.CostEstimate(flops=flops, bytes_accessed=1, transcendentals=0)


def params(mib=32, **more):
    return pltpu.CompilerParams(vmem_limit_bytes=mib * 1024 * 1024, **more)


def attend_block(q, keys, values, bias, factor, peak, summed):
    s = lax.dot_general(q, keys, (((1,), (1,)), ((), ())), preferred_element_type=F32)
    if bias is not None:
        s = s + bias
    high = jnp.max(s, axis=1, keepdims=True)
    high = high if peak is None else jnp.maximum(peak, high)
    w = jnp.exp2((s - high) * factor)
    o = jnp.dot(w.astype(BF16), values, preferred_element_type=F32)
    if peak is not None:
        o = summed * jnp.exp2((peak - high) * factor) + o
    return high, o


def near_kernel(factor, halves, seg_q, seg_k, q_ref, sk_ref, sv_ref, pk_ref, pv_ref, out_ref, stat_ref, bias, both):
    tokens, group = q_ref.shape[0], q_ref.shape[1] // HD

    @pl.when(pl.program_id(0) == 0)
    def _():
        same = seg_q[:, 0:1] == seg_k[0:1, :]
        last = seg_q[:, 1:2]
        where_k = lax.broadcasted_iota(jnp.int32, bias.shape, 1)
        bias[...] = jnp.where(same & (where_k <= last), 0.0, -1e30)
        both[:, HD:] = jnp.ones((both.shape[0], HD), BF16)

    @pl.when(pl.program_id(0) % halves == 0)
    def _():
        both[:tokens, :HD] = sv_ref[...]
        both[tokens:, :HD] = pv_ref[...]

    for h in range(group):
        q = q_ref[:, h * HD : (h + 1) * HD]
        peak, summed = attend_block(q, sk_ref[...], both[:tokens], bias[...], factor, None, None)
        peak, summed = attend_block(q, pk_ref[...], both[tokens:], None, factor, peak, summed)
        at = slice(h * HD, (h + 1) * HD)
        out_ref[:, at] = summed[:, :HD] / summed[:, HD:]
        stat_ref[:, at] = peak * factor + jnp.log2(summed[:, HD:])


def far_kernel(order, factor, halves, place, q_ref, near_ref, stat_ref, *refs):
    hops = len(order)
    below, above = refs[:hops], refs[hops : 2 * hops]
    out_ref, keys, both, held, sems = refs[2 * hops :]
    group = q_ref.shape[1] // HD
    rows = held.shape[1]
    slots = held.shape[2] // (2 * HD)
    slot = pl.program_id(0) // halves

    @pl.when(pl.program_id(0) == 0)
    def _():
        for step, choices in enumerate(order):
            for hop, from_below in sorted(set(choices)):
                here = functools.reduce(
                    jnp.logical_or,
                    [place[0] == i for i, c in enumerate(choices) if c == (hop, from_below)],
                )

                @pl.when(here)
                def _(ref=(below if from_below else above)[hop - 1], to=step):
                    pltpu.make_async_copy(ref, held.at[to], sems.at[to]).start()

        both[:, HD:] = jnp.ones((both.shape[0], HD), BF16)
        for i in range(hops):
            pltpu.make_async_copy(below[0], held.at[i], sems.at[i]).wait()

    @pl.when(pl.program_id(0) % halves == 0)
    def _():
        key_at = pl.ds(pl.multiple_of(slot * HD, HD), HD)
        value_at = pl.ds(pl.multiple_of((slots + slot) * HD, HD), HD)
        for i in range(hops):
            keys[i * rows : (i + 1) * rows] = held[i, :, key_at]
            both[i * rows : (i + 1) * rows, :HD] = held[i, :, value_at]

    for h in range(group):
        at = slice(h * HD, (h + 1) * HD)
        q = q_ref[:, at]
        peak, summed = None, None
        for i in range(hops):
            block = slice(i * rows, (i + 1) * rows)
            peak, summed = attend_block(q, keys[block], both[block], None, factor, peak, summed)
        far, near = jnp.broadcast_to(peak * factor, q.shape), stat_ref[:, at]
        high = jnp.maximum(far, near)
        far, near = jnp.exp2(far - high), jnp.exp2(near - high)
        result = summed[:, :HD] * far + near_ref[:, at] * near
        out_ref[:, at] = (result / (summed[:, HD:] * far + near)).astype(BF16)


FACTOR = math.log2(math.e) / math.sqrt(HD)


def attend_near(q, seg_q, seg_k, keys, values, prefix_keys, prefix_values):
    tokens, width = q.shape
    rows, slots = prefix_keys.shape[0], prefix_keys.shape[1] // HD
    halves = 2 if (width // slots // HD) % 2 == 0 else 1
    wide = width // slots // halves
    part = pl.BlockSpec((tokens, wide), lambda s: (0, s))
    one = lambda n: pl.BlockSpec((n, HD), lambda s: (0, s // halves))
    return pl.pallas_call(
        functools.partial(near_kernel, FACTOR, halves),
        grid=(slots * halves,),
        out_shape=[jax.ShapeDtypeStruct((tokens, width), F32)] * 2,
        in_specs=[
            pl.BlockSpec((tokens, 2), lambda s: (0, 0)),
            pl.BlockSpec((1, tokens), lambda s: (0, 0)),
            part,
            one(tokens),
            one(tokens),
            one(rows),
            one(rows),
        ],
        out_specs=[part] * 2,
        scratch_shapes=[
            pltpu.VMEM((tokens, tokens), F32),
            pltpu.VMEM((tokens + rows, 2 * HD), BF16),
        ],
        compiler_params=params(58),
        cost_estimate=cost(16 * tokens * (tokens + rows) * width),
        name="attend_near",
    )(seg_q, seg_k, q, keys, values, prefix_keys, prefix_values)


def attend_far(z, q, near, stats, below, above):
    tokens, width = q.shape
    rows, hops = below[0].shape[0], len(below)
    slots = below[0].shape[1] // (2 * HD)
    halves = 2 if (width // slots // HD) % 2 == 0 else 1
    part = pl.BlockSpec((tokens, width // slots // halves), lambda s: (0, s))
    anywhere = pl.BlockSpec(memory_space=pl.ANY)
    return pl.pallas_call(
        functools.partial(far_kernel, prefix_order(hops + 1), FACTOR, halves),
        grid=(slots * halves,),
        out_shape=jax.ShapeDtypeStruct((tokens, width), BF16),
        in_specs=[pl.BlockSpec(memory_space=SMEM), part, part, part] + [anywhere] * (2 * hops),
        out_specs=part,
        scratch_shapes=[
            pltpu.VMEM((hops * rows, HD), BF16),
            pltpu.VMEM((hops * rows, 2 * HD), BF16),
            pltpu.VMEM((hops,) + below[0].shape, BF16),
            pltpu.SemaphoreType.DMA((hops,)),
        ],
        compiler_params=params(58),
        cost_estimate=cost(16 * tokens * hops * rows * width),
        name="attend_far",
    )(z, q, near, stats, *below, *above)


def project_kernel(per_tile, wide, n_parts, which, *refs):
    a_refs, w_ref = refs[:n_parts], refs[n_parts]
    outs, done, sems = refs[n_parts + 1 : -2], refs[-2], refs[-1]
    step = pl.program_id(0)
    a = jnp.concatenate([ref[...] for ref in a_refs], axis=1)
    done[step] = jnp.dot(a, w_ref[...], preferred_element_type=F32).astype(BF16)

    def leaving(i):
        piece = done.at[i // per_tile, :, (i % per_tile) * wide : (i % per_tile + 1) * wide]
        return pltpu.make_async_copy(piece, outs[i], sems.at[i])

    for i in range(len(outs)):

        @pl.when(step == i // per_tile)
        def _(i=i):
            leaving(i).start()

    @pl.when(step == pl.num_programs(0) - 1)
    def _():
        for i in range(len(outs)):
            leaving(i).wait()


def project(parts, w, owners, count, pieces, weigh=0):
    rows, depth = parts[0].shape[0], w.shape[0]
    block = w.shape[1] // count
    wide = block // pieces
    tile = max(wide, min(1024, block))
    per_tile, tiles = tile // wide, block // tile
    n = owners.shape[0]
    return pl.pallas_call(
        functools.partial(project_kernel, per_tile, wide, len(parts)),
        out_shape=[jax.ShapeDtypeStruct((rows, wide), BF16)] * (n * pieces),
        grid_spec=pltpu.PrefetchScalarGridSpec(
            num_scalar_prefetch=1,
            grid=(n * tiles,),
            in_specs=[
                *[pl.BlockSpec(a.shape, lambda j, which: (0, 0)) for a in parts],
                pl.BlockSpec((depth, tile), lambda j, which: (0, which[j // tiles] * tiles + j % tiles)),
            ],
            out_specs=[pl.BlockSpec(memory_space=pl.ANY)] * (n * pieces),
            scratch_shapes=[
                pltpu.VMEM((n * tiles, rows, tile), BF16),
                pltpu.SemaphoreType.DMA((n * pieces,)),
            ],
        ),
        compiler_params=params(58),
        cost_estimate=cost(1 + weigh * n * rows * depth * block // 2),
        name="project",
    )(owners, *parts, w)


def add_kernel(n, *refs):
    for a, b, out in zip(refs[:n], refs[n : 2 * n], refs[2 * n :]):
        out[...] = (a[...].astype(F32) + b[...].astype(F32)).astype(BF16)


def add_all(first, second):
    n, (rows, wide) = len(first), first[0].shape
    block = pl.BlockSpec((rows // 4, wide), lambda i: (i, 0))
    return pl.pallas_call(
        functools.partial(add_kernel, n),
        grid=(4,),
        out_shape=[jax.ShapeDtypeStruct((rows, wide), BF16)] * n,
        in_specs=[block] * (2 * n),
        out_specs=[block] * n,
        compiler_params=params(58),
        cost_estimate=SMALL,
        name="add_all",
    )(*first, *second)


def most_slots(n_dp, requests):
    return sum(CAPS) + requests * (n_dp - 1) + n_dp


def schedule_kernel(n_dp, requests, per, idx_ref, z_ref, out_ref):
    limit = most_slots(n_dp, requests)
    links = n_dp - 1
    idx = idx_ref[...]
    shape = idx.shape
    z = z_ref[0]
    lane = lax.broadcasted_iota(jnp.int32, shape, 1)
    row = lax.broadcasted_iota(jnp.int32, shape, 0)
    link = lax.broadcasted_iota(jnp.int32, (links,) + shape, 0)
    valid = (lane < n_dp * requests) & (row < 4)
    down = (row % 2) == 1
    taker = (z + n_dp - lane // requests) % n_dp
    holder = idx // per
    local = idx % per
    own = valid & (taker == holder)
    dst = jnp.where(down, n_dp - 1 - taker, taker)
    src = jnp.where(down, n_dp - 1 - holder, holder)
    me = jnp.where(down, n_dp - 1 - z, z)
    moving = valid & (src < dst)
    dst = jnp.where(moving, dst, 0)
    pos = jnp.where(moving, src, 0)
    rank = dst * 256 + 255 - (taker * requests + lane % requests)
    zero = jnp.zeros(shape, jnp.int32)

    def one_round(first, slots, pos, came, codes):
        can = (pos[None] == link) & (dst[None] > link)
        code = jnp.where(src == me, local, per + came)
        moved = zero
        for slot in range(slots):
            key = jnp.where(can, rank[None], -1)
            best = jnp.max(key, axis=2, keepdims=True)
            chosen = can & (key == best)
            can = can & ~chosen
            sent = jnp.sum(jnp.where(chosen & (link == me[None]), code[None], 0), axis=0)
            codes = jnp.where(lane == first + slot, jnp.sum(sent, axis=1, keepdims=True), codes)
            got = jnp.sum(jnp.where(chosen & (link + 1 == me[None]), 1, 0), axis=0)
            came = jnp.where(got > 0, first + slot, came)
            moved = moved + jnp.sum(jnp.where(chosen, 1, 0), axis=0)
        return pos + moved, came, codes

    came, codes = zero, zero
    first = 0

    def left(pos):
        return jnp.max(jnp.where(pos < dst, 1, 0))

    unfinished = []
    for slots in CAPS:
        unfinished.append(left(pos))
        pos, came, codes = one_round(first, slots, pos, came, codes)
        first += slots

    def later(carry):
        k, _, pos, came, codes = carry
        pos, came, codes = one_round(k, 1, pos, came, codes)
        return k + 1, left(pos), pos, came, codes

    used, _, _, came, codes = lax.while_loop(
        lambda c: (c[1] > 0) & (c[0] < limit), later, (jnp.int32(first), left(pos), pos, came, codes)
    )
    used = jnp.where(unfinished[-1] > 0, used, first - CAPS[-1])
    place = jnp.where(own & (row == 0), local, 0)
    place = place + jnp.where(moving & (row == 0), per + came, 0)
    place = place + jnp.where(moving & (row == 1), per + limit + came, 0)
    place = jnp.sum(jnp.where(row < 2, place, 0), axis=0, keepdims=True)
    out = jnp.where(row < 2, codes, 0)
    out = jnp.where(row == 2, place, out)
    out_ref[...] = jnp.where(row == 3, used, out)


def make_schedule(n_dp, requests, per, idx_rows, z):
    return pl.pallas_call(
        functools.partial(schedule_kernel, n_dp, requests, per),
        out_shape=jax.ShapeDtypeStruct((8, 128), jnp.int32),
        in_specs=[pl.BlockSpec(memory_space=VMEM), pl.BlockSpec(memory_space=SMEM)],
        out_specs=pl.BlockSpec(memory_space=VMEM),
        cost_estimate=SMALL,
        name="schedule",
    )(idx_rows, z)


def slots_of(came):
    return [(r, j) for r, ref in enumerate(came) for j in range(CAPS[r])]


def fetch(code, per, own, ups, downs, limit, out, sems):
    rank = own[0].shape[1]

    @pl.when(code < per)
    def _():
        at = jnp.minimum(code, per - 1)
        for half in range(2):
            to = out.at[half * rank : (half + 1) * rank]
            pltpu.make_async_copy(own[half].at[at], to, sems.at[half]).start()

    for base, came in ((per, ups), (per + limit, downs)):
        for k, (r, j) in enumerate(slots_of(came)):

            @pl.when(code == base + k)
            def _(ref=came[r], j=j):
                for half in range(2):
                    part = slice(half * rank, (half + 1) * rank)
                    pltpu.make_async_copy(ref.at[j, part], out.at[part], sems.at[half]).start()


def fetched(own, out, sems):
    rank = own[0].shape[1]
    for half in range(2):
        to = out.at[half * rank : (half + 1) * rank]
        pltpu.make_async_copy(own[half].at[0], to, sems.at[half]).wait()


def pick_kernel(first, count, per, limit, n_came, sched, down_ref, up_ref, *refs):
    ups, downs = refs[:n_came], refs[n_came : 2 * n_came]
    outs, sems = refs[2 * n_came : -1], refs[-1]
    own = (down_ref, up_ref)
    for i in range(count):
        for way, came in enumerate((ups, downs)):
            code = sched[way, first + i]
            fetch(code, per, own, came, (), limit, outs[way].at[i], sems.at[way, i])
    for i in range(count):
        for way in range(2):
            fetched(own, outs[way].at[i], sems.at[way, i])


def slot_shape(own):
    return (2 * own[0].shape[1], own[0].shape[2])


def pick_sends(sched, own, ups, downs, number, limit):
    count, first = CAPS[number], sum(CAPS[:number])
    anywhere = pl.BlockSpec(memory_space=pl.ANY)
    in_vmem = pl.BlockSpec(memory_space=VMEM)
    out = jax.ShapeDtypeStruct((count,) + slot_shape(own), BF16)
    return pl.pallas_call(
        functools.partial(pick_kernel, first, count, own[0].shape[0], limit, len(ups)),
        out_shape=[out] * 2,
        in_specs=[pl.BlockSpec(memory_space=SMEM)] + [anywhere] * (2 + 2 * len(ups)),
        out_specs=[in_vmem] * 2,
        scratch_shapes=[pltpu.SemaphoreType.DMA((2, count, 2))],
        compiler_params=params(16),
        cost_estimate=SMALL,
        name="pick",
    )(sched, *own, *ups, *downs)


def gather_kernel(per, limit, requests, n_came, sched, z, down_ref, up_ref, *refs):
    ups, downs = refs[:n_came], refs[n_came : 2 * n_came]
    out, sems = refs[-2], refs[-1]
    own = (down_ref, up_ref)
    for r in range(requests):
        code = sched[2, r]
        fetch(code, per, own, ups, downs, limit, out.at[r], sems.at[r])
    for r in range(requests):
        fetched(own, out.at[r], sems.at[r])


def gather_own(sched, z, own, ups, downs, requests, limit):
    anywhere = pl.BlockSpec(memory_space=pl.ANY)
    return pl.pallas_call(
        functools.partial(gather_kernel, own[0].shape[0], limit, requests, len(ups)),
        out_shape=jax.ShapeDtypeStruct((requests,) + slot_shape(own), BF16),
        in_specs=[pl.BlockSpec(memory_space=SMEM)] * 2 + [anywhere] * (2 + 2 * len(ups)),
        out_specs=pl.BlockSpec(memory_space=VMEM),
        scratch_shapes=[pltpu.SemaphoreType.DMA((requests, 2))],
        compiler_params=params(16),
        cost_estimate=SMALL,
        name="gather_own",
    )(sched, z, *own, *ups, *downs)


def later_rounds(sched, z, own, ups, downs, requests, limit, n_dp):
    up, down = line(n_dp)
    per = own[0].shape[0]
    made = sum(CAPS)
    spare = jnp.zeros((limit - made,) + slot_shape(own), BF16)
    up_all = jnp.concatenate([*ups, spare])
    down_all = jnp.concatenate([*downs, spare])

    def choose(code, came):
        at = jnp.minimum(code, per - 1)
        held = [lax.dynamic_index_in_dim(o, at, 0, keepdims=False) for o in own]
        passed = lax.dynamic_index_in_dim(came, jnp.clip(code - per, 0, limit - 1), 0, keepdims=False)
        return jnp.where(code < per, jnp.concatenate(held), passed)

    def step(carry):
        k, up_all, down_all = carry
        from_below = lax.ppermute(choose(sched[0, k], up_all), "dp", up)
        from_above = lax.ppermute(choose(sched[1, k], down_all), "dp", down)
        up_all = lax.dynamic_update_index_in_dim(up_all, from_below, k, 0)
        down_all = lax.dynamic_update_index_in_dim(down_all, from_above, k, 0)
        return k + 1, up_all, down_all

    _, up_all, down_all = lax.while_loop(
        lambda c: c[0] < sched[3, 0], step, (jnp.int32(made), up_all, down_all)
    )
    places = sched[2]
    picked = []
    for r in range(requests):
        code = places[r]
        below = choose(code, up_all)
        above = lax.dynamic_index_in_dim(
            down_all, jnp.clip(code - per - limit, 0, limit - 1), 0, keepdims=False
        )
        picked.append(jnp.where(code >= per + limit, above, below))
    return jnp.stack(picked)


def line(n):
    return [(i, i + 1) for i in range(n - 1)], [(i + 1, i) for i in range(n - 1)]


def adapter_round(sched, own, ups, downs, requests, n_dp, after=None):
    up, down = line(n_dp)
    sends = pick_sends(sched, own, ups, downs, len(ups), most_slots(n_dp, requests))
    sends, after = lax.optimization_barrier((sends, after))
    ups = ups + [lax.ppermute(sends[0], "dp", up)]
    downs = downs + [lax.ppermute(sends[1], "dp", down)]
    return ups, downs, after


def last_adapters(sched, z, own, ups, downs, requests, n_dp):
    limit = most_slots(n_dp, requests)

    def one_round():
        return adapter_round(sched, own, ups, downs, requests, n_dp)[:2]

    def enough():
        return gather_own(sched, z, own, ups, downs, requests, limit)

    def one_more():
        return gather_own(sched, z, own, *one_round(), requests, limit)

    def many_more():
        return later_rounds(sched, z, own, *one_round(), requests, limit, n_dp)

    used = sched[3, 0]
    short = (used > sum(CAPS[:-1])).astype(jnp.int32) + (used > sum(CAPS)).astype(jnp.int32)
    return lax.switch(short, (enough, one_more, many_more))


def by_core(n):
    return [(i, i ^ 1) for i in range(n)]


def by_chip(n):
    return [(i, i ^ 2) for i in range(n)]


def added(a, b):
    return (a.astype(F32) + b.astype(F32)).astype(BF16)


def all_sum(x, n_tensor):
    if n_tensor != 4:
        return lax.psum(x, "tensor")
    x = added(x, lax.ppermute(x, "tensor", by_core(n_tensor)))
    return added(x, lax.ppermute(x, "tensor", by_chip(n_tensor)))


def prefix_order(n):
    table = []
    for z in range(n):
        seen = []
        for hop in range(1, n):
            seen += [(hop, True)] if hop <= z else []
            seen += [(hop, False)] if hop <= n - 1 - z else []
        table.append(seen)
    return [[table[z][s] for z in range(n)] for s in range(n - 1)]


def per_device(
    n_groups,
    n_dp,
    n_tensor,
    queries,
    suffix_rotated_key_slots,
    suffix_value_slots,
    shared_prefix_key_slots,
    shared_prefix_value_slots,
    lengths,
    request_adapter_index,
    output_weight_matrix,
    adapter_down_factors,
    adapter_up_factors,
):
    tokens, width = queries.shape
    requests = lengths.shape[1]
    per = adapter_down_factors.shape[0]
    zi = lax.axis_index("dp").astype(jnp.int32)
    z = zi.reshape(1)
    ti = lax.axis_index("tensor").astype(jnp.int32)
    up, down = line(n_dp)

    own_rows = jnp.concatenate([shared_prefix_key_slots, shared_prefix_value_slots], axis=1)
    below, above = [own_rows], [own_rows]
    hop_first = (lax.ppermute(own_rows, "dp", up), lax.ppermute(own_rows, "dp", down))

    known = jnp.concatenate(
        [request_adapter_index]
        + [
            lax.ppermute(request_adapter_index, "dp", [(i, (i + s) % n_dp) for i in range(n_dp)])
            for s in range(1, n_dp)
        ],
        axis=1,
    )

    position = jnp.arange(tokens, dtype=jnp.int32)
    seg_ends = jnp.cumsum(lengths[0])
    request_of = jnp.sum((position[:, None] >= seg_ends[None, :]).astype(jnp.int32), axis=1)
    seg_q = jnp.stack([request_of, position], axis=1)
    seg_k = request_of[None]
    hop_first, known = lax.optimization_barrier((hop_first, known))
    queries_here, hop_first = lax.optimization_barrier((queries, hop_first))
    near = attend_near(
        queries_here,
        seg_q,
        seg_k,
        suffix_rotated_key_slots,
        suffix_value_slots,
        shared_prefix_key_slots,
        shared_prefix_value_slots,
    )
    other = lax.ppermute(known, "groups", [(i, (i + 1) % n_groups) for i in range(n_groups)])
    rows = jnp.concatenate([known, known, other, other], axis=0)
    idx_rows = jnp.pad(rows, ((0, 8 - rows.shape[0]), (0, 128 - rows.shape[1])))
    for hop in range(1, n_dp):
        if hop == 1:
            from_below, from_above = hop_first
        else:
            from_below, from_above = below[-1], above[-1]
            if hop == 3:
                from_below, from_above, near, idx_rows = lax.optimization_barrier(
                    (from_below, from_above, near, idx_rows)
                )
            from_below = lax.ppermute(from_below, "dp", up[hop - 1 :])
            from_above = lax.ppermute(from_above, "dp", down[: n_dp - hop])
        below.append(from_below)
        above.append(from_above)

    own = (jnp.transpose(adapter_down_factors, (0, 2, 1)), adapter_up_factors)
    sched = make_schedule(n_dp, requests, per, idx_rows, z)
    if n_dp > 2:
        sched, below[2], above[2] = lax.optimization_barrier((sched, below[2], above[2]))
    ups, downs, near = adapter_round(sched, own, [], [], requests, n_dp, near)
    attended = attend_far(z, queries, *near, below[1:], above[1:])
    ups, downs, attended = adapter_round(sched, own, ups, downs, requests, n_dp, attended)
    if n_tensor == 4:
        core, chip = by_core(n_tensor), by_chip(n_tensor)

        def share(parts, owners, weigh):
            return project([parts], output_weight_matrix, jnp.stack(owners), n_tensor, PIECES, weigh)

        far = share(attended, (ti ^ 3, ti ^ 2), 8)
        far_other, far_same = far[:PIECES], far[PIECES:]
        far_other, ups, downs = lax.optimization_barrier((far_other, ups, downs))
        from_core = [lax.ppermute(x, "tensor", core) for x in far_other]
        sends = add_all(far_same, from_core)
        sched, sends = lax.optimization_barrier((sched, sends))
        arriving = [lax.ppermute(x, "tensor", chip) for x in sends]
    ups, downs, again = adapter_round(sched, own, ups, downs, requests, n_dp, attended)
    if n_tensor == 4:
        near = share(again, (ti ^ 1, ti), 4)
        near_other, near_same = near[:PIECES], near[PIECES:]
        near_from_core = [lax.ppermute(x, "tensor", core) for x in near_other]
        sched, arriving[:2] = lax.optimization_barrier((sched, arriving[:2]))
    picked = last_adapters(sched, z, own, ups, downs, requests, n_dp)
    if n_tensor == 4:
        picked, arriving[2:-1] = lax.optimization_barrier((picked, arriving[2:-1]))
    rank = picked.shape[1] // 2
    picked_down, picked_up = picked[:, :rank], picked[:, rank:]
    select = request_of[:, None] == jnp.arange(requests, dtype=jnp.int32)[None, :]
    first = lax.dot_general(
        attended,
        picked_down.reshape(-1, width),
        (((1,), (1,)), ((), ())),
        preferred_element_type=F32,
    ).reshape(tokens, requests, -1)
    partial_shrink = jnp.sum(jnp.where(select[:, :, None], first, 0.0), axis=1).astype(BF16)
    if n_tensor == 4:
        bases = [
            mine.astype(F32) + near.astype(F32) + far.astype(F32)
            for mine, near, far in zip(near_same, near_from_core, arriving)
        ]
        base = jnp.concatenate(bases, axis=1)
    else:
        (whole,) = project([attended], output_weight_matrix, jnp.zeros((1,), jnp.int32), 1, 1)
        share = lax.psum_scatter(whole, "tensor", scatter_dimension=1, tiled=True)
        base = share.astype(F32)
    shrink = all_sum(partial_shrink, n_tensor)
    spread = jnp.where(select[:, :, None], shrink[:, None, :], 0).reshape(tokens, -1)
    expand = jnp.dot(
        spread, picked_up.reshape(spread.shape[1], -1), preferred_element_type=F32
    )
    return (base + expand).astype(BF16)


def solution(mesh):
    return jax.shard_map(
        functools.partial(
            per_device, mesh.shape["groups"], mesh.shape["dp"], mesh.shape["tensor"]
        ),
        mesh=mesh,
        in_specs=(
            P(("groups", "dp"), "tensor"),
            P(("groups", "dp"), "tensor"),
            P(("groups", "dp"), "tensor"),
            P(("groups", "dp"), "tensor"),
            P(("groups", "dp"), "tensor"),
            P(("groups", "dp"), None),
            P(("groups", "dp"), None),
            P("tensor", None),
            P("dp", "tensor", None),
            P("dp", None, "tensor"),
        ),
        out_specs=P(("groups", "dp"), "tensor"),
        check_vma=False,
    )
```

```python
import functools
import math

import jax
import jax.numpy as jnp
from jax import lax
from jax.experimental import pallas as pl
from jax.experimental.pallas import tpu as pltpu
from jax.sharding import PartitionSpec as P

HD = 128
CAPS = (2, 2, 2, 1)
PIECES = 4
SMALL = pl.CostEstimate(flops=1, bytes_accessed=1, transcendentals=0)
F32 = jnp.float32
BF16 = jnp.bfloat16
SMEM = pltpu.MemorySpace.SMEM
VMEM = pltpu.MemorySpace.VMEM


def cost(flops):
    return pl.CostEstimate(flops=flops, bytes_accessed=1, transcendentals=0)


def params(mib=32, **more):
    return pltpu.CompilerParams(vmem_limit_bytes=mib * 1024 * 1024, **more)


def attend_block(q, keys, values, bias, factor, peak, summed):
    s = lax.dot_general(q, keys, (((1,), (1,)), ((), ())), preferred_element_type=F32)
    if bias is not None:
        s = s + bias
    high = jnp.max(s, axis=1, keepdims=True)
    high = high if peak is None else jnp.maximum(peak, high)
    w = jnp.exp2((s - high) * factor)
    o = jnp.dot(w.astype(BF16), values, preferred_element_type=F32)
    if peak is not None:
        o = summed * jnp.exp2((peak - high) * factor) + o
    return high, o


def near_kernel(factor, halves, seg_q, seg_k, q_ref, sk_ref, sv_ref, pk_ref, pv_ref, out_ref, stat_ref, bias, both):
    tokens, group = q_ref.shape[0], q_ref.shape[1] // HD

    @pl.when(pl.program_id(0) == 0)
    def _():
        same = seg_q[:, 0:1] == seg_k[0:1, :]
        last = seg_q[:, 1:2]
        where_k = lax.broadcasted_iota(jnp.int32, bias.shape, 1)
        bias[...] = jnp.where(same & (where_k <= last), 0.0, -1e30)
        both[:, HD:] = jnp.ones((both.shape[0], HD), BF16)

    @pl.when(pl.program_id(0) % halves == 0)
    def _():
        both[:tokens, :HD] = sv_ref[...]
        both[tokens:, :HD] = pv_ref[...]

    for h in range(group):
        q = q_ref[:, h * HD : (h + 1) * HD]
        peak, summed = attend_block(q, sk_ref[...], both[:tokens], bias[...], factor, None, None)
        peak, summed = attend_block(q, pk_ref[...], both[tokens:], None, factor, peak, summed)
        at = slice(h * HD, (h + 1) * HD)
        out_ref[:, at] = summed[:, :HD] / summed[:, HD:]
        stat_ref[:, at] = peak * factor + jnp.log2(summed[:, HD:])


def far_kernel(order, factor, halves, place, q_ref, near_ref, stat_ref, *refs):
    hops = len(order)
    below, above = refs[:hops], refs[hops : 2 * hops]
    out_ref, keys, both, held, sems = refs[2 * hops :]
    group = q_ref.shape[1] // HD
    rows = held.shape[1]
    slots = held.shape[2] // (2 * HD)
    slot = pl.program_id(0) // halves

    @pl.when(pl.program_id(0) == 0)
    def _():
        for step, choices in enumerate(order):
            for hop, from_below in sorted(set(choices)):
                here = functools.reduce(
                    jnp.logical_or,
                    [place[0] == i for i, c in enumerate(choices) if c == (hop, from_below)],
                )

                @pl.when(here)
                def _(ref=(below if from_below else above)[hop - 1], to=step):
                    pltpu.make_async_copy(ref, held.at[to], sems.at[to]).start()

        both[:, HD:] = jnp.ones((both.shape[0], HD), BF16)
        for i in range(hops):
            pltpu.make_async_copy(below[0], held.at[i], sems.at[i]).wait()

    @pl.when(pl.program_id(0) % halves == 0)
    def _():
        key_at = pl.ds(pl.multiple_of(slot * HD, HD), HD)
        value_at = pl.ds(pl.multiple_of((slots + slot) * HD, HD), HD)
        for i in range(hops):
            keys[i * rows : (i + 1) * rows] = held[i, :, key_at]
            both[i * rows : (i + 1) * rows, :HD] = held[i, :, value_at]

    for h in range(group):
        at = slice(h * HD, (h + 1) * HD)
        q = q_ref[:, at]
        peak, summed = None, None
        for i in range(hops):
            block = slice(i * rows, (i + 1) * rows)
            peak, summed = attend_block(q, keys[block], both[block], None, factor, peak, summed)
        far, near = jnp.broadcast_to(peak * factor, q.shape), stat_ref[:, at]
        high = jnp.maximum(far, near)
        far, near = jnp.exp2(far - high), jnp.exp2(near - high)
        result = summed[:, :HD] * far + near_ref[:, at] * near
        out_ref[:, at] = (result / (summed[:, HD:] * far + near)).astype(BF16)


FACTOR = math.log2(math.e) / math.sqrt(HD)


def attend_near(q, seg_q, seg_k, keys, values, prefix_keys, prefix_values):
    tokens, width = q.shape
    rows, slots = prefix_keys.shape[0], prefix_keys.shape[1] // HD
    halves = 2 if (width // slots // HD) % 2 == 0 else 1
    wide = width // slots // halves
    part = pl.BlockSpec((tokens, wide), lambda s: (0, s))
    one = lambda n: pl.BlockSpec((n, HD), lambda s: (0, s // halves))
    return pl.pallas_call(
        functools.partial(near_kernel, FACTOR, halves),
        grid=(slots * halves,),
        out_shape=[jax.ShapeDtypeStruct((tokens, width), F32)] * 2,
        in_specs=[
            pl.BlockSpec((tokens, 2), lambda s: (0, 0)),
            pl.BlockSpec((1, tokens), lambda s: (0, 0)),
            part,
            one(tokens),
            one(tokens),
            one(rows),
            one(rows),
        ],
        out_specs=[part] * 2,
        scratch_shapes=[
            pltpu.VMEM((tokens, tokens), F32),
            pltpu.VMEM((tokens + rows, 2 * HD), BF16),
        ],
        compiler_params=params(58),
        cost_estimate=cost(16 * tokens * (tokens + rows) * width),
        name="attend_near",
    )(seg_q, seg_k, q, keys, values, prefix_keys, prefix_values)


def attend_far(z, q, near, stats, below, above):
    tokens, width = q.shape
    rows, hops = below[0].shape[0], len(below)
    slots = below[0].shape[1] // (2 * HD)
    halves = 2 if (width // slots // HD) % 2 == 0 else 1
    part = pl.BlockSpec((tokens, width // slots // halves), lambda s: (0, s))
    anywhere = pl.BlockSpec(memory_space=pl.ANY)
    return pl.pallas_call(
        functools.partial(far_kernel, prefix_order(hops + 1), FACTOR, halves),
        grid=(slots * halves,),
        out_shape=jax.ShapeDtypeStruct((tokens, width), BF16),
        in_specs=[pl.BlockSpec(memory_space=SMEM), part, part, part] + [anywhere] * (2 * hops),
        out_specs=part,
        scratch_shapes=[
            pltpu.VMEM((hops * rows, HD), BF16),
            pltpu.VMEM((hops * rows, 2 * HD), BF16),
            pltpu.VMEM((hops,) + below[0].shape, BF16),
            pltpu.SemaphoreType.DMA((hops,)),
        ],
        compiler_params=params(58),
        cost_estimate=cost(16 * tokens * hops * rows * width),
        name="attend_far",
    )(z, q, near, stats, *below, *above)


def project_kernel(per_tile, wide, n_parts, which, *refs):
    a_refs, w_ref = refs[:n_parts], refs[n_parts]
    outs, done, sems = refs[n_parts + 1 : -2], refs[-2], refs[-1]
    step = pl.program_id(0)
    a = jnp.concatenate([ref[...] for ref in a_refs], axis=1)
    done[step] = jnp.dot(a, w_ref[...], preferred_element_type=F32).astype(BF16)

    def leaving(i):
        piece = done.at[i // per_tile, :, (i % per_tile) * wide : (i % per_tile + 1) * wide]
        return pltpu.make_async_copy(piece, outs[i], sems.at[i])

    for i in range(len(outs)):

        @pl.when(step == i // per_tile)
        def _(i=i):
            leaving(i).start()

    @pl.when(step == pl.num_programs(0) - 1)
    def _():
        for i in range(len(outs)):
            leaving(i).wait()


def project(parts, w, owners, count, pieces, weigh=0):
    rows, depth = parts[0].shape[0], w.shape[0]
    block = w.shape[1] // count
    wide = block // pieces
    tile = max(wide, min(1024, block))
    per_tile, tiles = tile // wide, block // tile
    n = owners.shape[0]
    return pl.pallas_call(
        functools.partial(project_kernel, per_tile, wide, len(parts)),
        out_shape=[jax.ShapeDtypeStruct((rows, wide), BF16)] * (n * pieces),
        grid_spec=pltpu.PrefetchScalarGridSpec(
            num_scalar_prefetch=1,
            grid=(n * tiles,),
            in_specs=[
                *[pl.BlockSpec(a.shape, lambda j, which: (0, 0)) for a in parts],
                pl.BlockSpec((depth, tile), lambda j, which: (0, which[j // tiles] * tiles + j % tiles)),
            ],
            out_specs=[pl.BlockSpec(memory_space=pl.ANY)] * (n * pieces),
            scratch_shapes=[
                pltpu.VMEM((n * tiles, rows, tile), BF16),
                pltpu.SemaphoreType.DMA((n * pieces,)),
            ],
        ),
        compiler_params=params(58),
        cost_estimate=cost(1 + weigh * n * rows * depth * block // 2),
        name="project",
    )(owners, *parts, w)


def add_kernel(n, *refs):
    for a, b, out in zip(refs[:n], refs[n : 2 * n], refs[2 * n :]):
        out[...] = (a[...].astype(F32) + b[...].astype(F32)).astype(BF16)


def add_all(first, second):
    n, (rows, wide) = len(first), first[0].shape
    block = pl.BlockSpec((rows // 4, wide), lambda i: (i, 0))
    return pl.pallas_call(
        functools.partial(add_kernel, n),
        grid=(4,),
        out_shape=[jax.ShapeDtypeStruct((rows, wide), BF16)] * n,
        in_specs=[block] * (2 * n),
        out_specs=[block] * n,
        compiler_params=params(58),
        cost_estimate=SMALL,
        name="add_all",
    )(*first, *second)


def most_slots(n_dp, requests):
    return sum(CAPS) + requests * (n_dp - 1) + n_dp


def schedule_kernel(n_dp, requests, per, idx_ref, z_ref, out_ref):
    limit = most_slots(n_dp, requests)
    links = n_dp - 1
    idx = idx_ref[...]
    shape = idx.shape
    z = z_ref[0]
    lane = lax.broadcasted_iota(jnp.int32, shape, 1)
    row = lax.broadcasted_iota(jnp.int32, shape, 0)
    link = lax.broadcasted_iota(jnp.int32, (links,) + shape, 0)
    valid = (lane < n_dp * requests) & (row < 4)
    down = (row % 2) == 1
    taker = (z + n_dp - lane // requests) % n_dp
    holder = idx // per
    local = idx % per
    own = valid & (taker == holder)
    dst = jnp.where(down, n_dp - 1 - taker, taker)
    src = jnp.where(down, n_dp - 1 - holder, holder)
    me = jnp.where(down, n_dp - 1 - z, z)
    moving = valid & (src < dst)
    dst = jnp.where(moving, dst, 0)
    pos = jnp.where(moving, src, 0)
    rank = dst * 256 + 255 - (taker * requests + lane % requests)
    zero = jnp.zeros(shape, jnp.int32)

    def one_round(first, slots, pos, came, codes):
        can = (pos[None] == link) & (dst[None] > link)
        code = jnp.where(src == me, local, per + came)
        moved = zero
        for slot in range(slots):
            key = jnp.where(can, rank[None], -1)
            best = jnp.max(key, axis=2, keepdims=True)
            chosen = can & (key == best)
            can = can & ~chosen
            sent = jnp.sum(jnp.where(chosen & (link == me[None]), code[None], 0), axis=0)
            codes = jnp.where(lane == first + slot, jnp.sum(sent, axis=1, keepdims=True), codes)
            got = jnp.sum(jnp.where(chosen & (link + 1 == me[None]), 1, 0), axis=0)
            came = jnp.where(got > 0, first + slot, came)
            moved = moved + jnp.sum(jnp.where(chosen, 1, 0), axis=0)
        return pos + moved, came, codes

    came, codes = zero, zero
    first = 0

    def left(pos):
        return jnp.max(jnp.where(pos < dst, 1, 0))

    unfinished = []
    for slots in CAPS:
        unfinished.append(left(pos))
        pos, came, codes = one_round(first, slots, pos, came, codes)
        first += slots

    def later(carry):
        k, _, pos, came, codes = carry
        pos, came, codes = one_round(k, 1, pos, came, codes)
        return k + 1, left(pos), pos, came, codes

    used, _, _, came, codes = lax.while_loop(
        lambda c: (c[1] > 0) & (c[0] < limit), later, (jnp.int32(first), left(pos), pos, came, codes)
    )
    used = jnp.where(unfinished[-1] > 0, used, first - CAPS[-1])
    place = jnp.where(own & (row == 0), local, 0)
    place = place + jnp.where(moving & (row == 0), per + came, 0)
    place = place + jnp.where(moving & (row == 1), per + limit + came, 0)
    place = jnp.sum(jnp.where(row < 2, place, 0), axis=0, keepdims=True)
    out = jnp.where(row < 2, codes, 0)
    out = jnp.where(row == 2, place, out)
    out_ref[...] = jnp.where(row == 3, used, out)


def make_schedule(n_dp, requests, per, idx_rows, z):
    return pl.pallas_call(
        functools.partial(schedule_kernel, n_dp, requests, per),
        out_shape=jax.ShapeDtypeStruct((8, 128), jnp.int32),
        in_specs=[pl.BlockSpec(memory_space=VMEM), pl.BlockSpec(memory_space=SMEM)],
        out_specs=pl.BlockSpec(memory_space=VMEM),
        cost_estimate=SMALL,
        name="schedule",
    )(idx_rows, z)


def slots_of(came):
    return [(r, j) for r, ref in enumerate(came) for j in range(CAPS[r])]


def fetch(code, per, own, ups, downs, limit, out, sems):
    rank = own[0].shape[1]

    @pl.when(code < per)
    def _():
        at = jnp.minimum(code, per - 1)
        for half in range(2):
            to = out.at[half * rank : (half + 1) * rank]
            pltpu.make_async_copy(own[half].at[at], to, sems.at[half]).start()

    for base, came in ((per, ups), (per + limit, downs)):
        for k, (r, j) in enumerate(slots_of(came)):

            @pl.when(code == base + k)
            def _(ref=came[r], j=j):
                for half in range(2):
                    part = slice(half * rank, (half + 1) * rank)
                    pltpu.make_async_copy(ref.at[j, part], out.at[part], sems.at[half]).start()


def fetched(own, out, sems):
    rank = own[0].shape[1]
    for half in range(2):
        to = out.at[half * rank : (half + 1) * rank]
        pltpu.make_async_copy(own[half].at[0], to, sems.at[half]).wait()


def pick_kernel(first, count, per, limit, n_came, sched, down_ref, up_ref, *refs):
    ups, downs = refs[:n_came], refs[n_came : 2 * n_came]
    outs, sems = refs[2 * n_came : -1], refs[-1]
    own = (down_ref, up_ref)
    for i in range(count):
        for way, came in enumerate((ups, downs)):
            code = sched[way, first + i]
            fetch(code, per, own, came, (), limit, outs[way].at[i], sems.at[way, i])
    for i in range(count):
        for way in range(2):
            fetched(own, outs[way].at[i], sems.at[way, i])


def slot_shape(own):
    return (2 * own[0].shape[1], own[0].shape[2])


def pick_sends(sched, own, ups, downs, number, limit):
    count, first = CAPS[number], sum(CAPS[:number])
    anywhere = pl.BlockSpec(memory_space=pl.ANY)
    in_vmem = pl.BlockSpec(memory_space=VMEM)
    out = jax.ShapeDtypeStruct((count,) + slot_shape(own), BF16)
    return pl.pallas_call(
        functools.partial(pick_kernel, first, count, own[0].shape[0], limit, len(ups)),
        out_shape=[out] * 2,
        in_specs=[pl.BlockSpec(memory_space=SMEM)] + [anywhere] * (2 + 2 * len(ups)),
        out_specs=[in_vmem] * 2,
        scratch_shapes=[pltpu.SemaphoreType.DMA((2, count, 2))],
        compiler_params=params(16),
        cost_estimate=SMALL,
        name="pick",
    )(sched, *own, *ups, *downs)


def gather_kernel(per, limit, requests, n_came, sched, z, down_ref, up_ref, *refs):
    ups, downs = refs[:n_came], refs[n_came : 2 * n_came]
    out, sems = refs[-2], refs[-1]
    own = (down_ref, up_ref)
    for r in range(requests):
        code = sched[2, r]
        fetch(code, per, own, ups, downs, limit, out.at[r], sems.at[r])
    for r in range(requests):
        fetched(own, out.at[r], sems.at[r])


def gather_own(sched, z, own, ups, downs, requests, limit):
    anywhere = pl.BlockSpec(memory_space=pl.ANY)
    return pl.pallas_call(
        functools.partial(gather_kernel, own[0].shape[0], limit, requests, len(ups)),
        out_shape=jax.ShapeDtypeStruct((requests,) + slot_shape(own), BF16),
        in_specs=[pl.BlockSpec(memory_space=SMEM)] * 2 + [anywhere] * (2 + 2 * len(ups)),
        out_specs=pl.BlockSpec(memory_space=VMEM),
        scratch_shapes=[pltpu.SemaphoreType.DMA((requests, 2))],
        compiler_params=params(16),
        cost_estimate=SMALL,
        name="gather_own",
    )(sched, z, *own, *ups, *downs)


def later_rounds(sched, z, own, ups, downs, requests, limit, n_dp):
    up, down = line(n_dp)
    per = own[0].shape[0]
    made = sum(CAPS)
    spare = jnp.zeros((limit - made,) + slot_shape(own), BF16)
    up_all = jnp.concatenate([*ups, spare])
    down_all = jnp.concatenate([*downs, spare])

    def choose(code, came):
        at = jnp.minimum(code, per - 1)
        held = [lax.dynamic_index_in_dim(o, at, 0, keepdims=False) for o in own]
        passed = lax.dynamic_index_in_dim(came, jnp.clip(code - per, 0, limit - 1), 0, keepdims=False)
        return jnp.where(code < per, jnp.concatenate(held), passed)

    def step(carry):
        k, up_all, down_all = carry
        from_below = lax.ppermute(choose(sched[0, k], up_all), "dp", up)
        from_above = lax.ppermute(choose(sched[1, k], down_all), "dp", down)
        up_all = lax.dynamic_update_index_in_dim(up_all, from_below, k, 0)
        down_all = lax.dynamic_update_index_in_dim(down_all, from_above, k, 0)
        return k + 1, up_all, down_all

    _, up_all, down_all = lax.while_loop(
        lambda c: c[0] < sched[3, 0], step, (jnp.int32(made), up_all, down_all)
    )
    places = sched[2]
    picked = []
    for r in range(requests):
        code = places[r]
        below = choose(code, up_all)
        above = lax.dynamic_index_in_dim(
            down_all, jnp.clip(code - per - limit, 0, limit - 1), 0, keepdims=False
        )
        picked.append(jnp.where(code >= per + limit, above, below))
    return jnp.stack(picked)


def line(n):
    return [(i, i + 1) for i in range(n - 1)], [(i + 1, i) for i in range(n - 1)]


def adapter_round(sched, own, ups, downs, requests, n_dp, after=None):
    up, down = line(n_dp)
    sends = pick_sends(sched, own, ups, downs, len(ups), most_slots(n_dp, requests))
    sends, after = lax.optimization_barrier((sends, after))
    ups = ups + [lax.ppermute(sends[0], "dp", up)]
    downs = downs + [lax.ppermute(sends[1], "dp", down)]
    return ups, downs, after


def last_adapters(sched, z, own, ups, downs, requests, n_dp):
    limit = most_slots(n_dp, requests)

    def one_round():
        return adapter_round(sched, own, ups, downs, requests, n_dp)[:2]

    def enough():
        return gather_own(sched, z, own, ups, downs, requests, limit)

    def one_more():
        return gather_own(sched, z, own, *one_round(), requests, limit)

    def many_more():
        return later_rounds(sched, z, own, *one_round(), requests, limit, n_dp)

    used = sched[3, 0]
    short = (used > sum(CAPS[:-1])).astype(jnp.int32) + (used > sum(CAPS)).astype(jnp.int32)
    return lax.switch(short, (enough, one_more, many_more))


def by_core(n):
    return [(i, i ^ 1) for i in range(n)]


def by_chip(n):
    return [(i, i ^ 2) for i in range(n)]


def added(a, b):
    return (a.astype(F32) + b.astype(F32)).astype(BF16)


def all_sum(x, n_tensor):
    if n_tensor != 4:
        return lax.psum(x, "tensor")
    x = added(x, lax.ppermute(x, "tensor", by_core(n_tensor)))
    return added(x, lax.ppermute(x, "tensor", by_chip(n_tensor)))


def prefix_order(n):
    table = []
    for z in range(n):
        seen = []
        for hop in range(1, n):
            seen += [(hop, True)] if hop <= z else []
            seen += [(hop, False)] if hop <= n - 1 - z else []
        table.append(seen)
    return [[table[z][s] for z in range(n)] for s in range(n - 1)]


def per_device(
    n_groups,
    n_dp,
    n_tensor,
    queries,
    suffix_rotated_key_slots,
    suffix_value_slots,
    shared_prefix_key_slots,
    shared_prefix_value_slots,
    lengths,
    request_adapter_index,
    output_weight_matrix,
    adapter_down_factors,
    adapter_up_factors,
):
    tokens, width = queries.shape
    requests = lengths.shape[1]
    per = adapter_down_factors.shape[0]
    zi = lax.axis_index("dp").astype(jnp.int32)
    z = zi.reshape(1)
    ti = lax.axis_index("tensor").astype(jnp.int32)
    up, down = line(n_dp)

    own_rows = jnp.concatenate([shared_prefix_key_slots, shared_prefix_value_slots], axis=1)
    below, above = [own_rows], [own_rows]

    known = jnp.concatenate(
        [request_adapter_index]
        + [
            lax.ppermute(request_adapter_index, "dp", [(i, (i + s) % n_dp) for i in range(n_dp)])
            for s in range(1, n_dp)
        ],
        axis=1,
    )

    own_rows, known = lax.optimization_barrier((own_rows, known))
    below, above = [own_rows], [own_rows]
    hop_first = (lax.ppermute(own_rows, "dp", up), lax.ppermute(own_rows, "dp", down))

    position = jnp.arange(tokens, dtype=jnp.int32)
    seg_ends = jnp.cumsum(lengths[0])
    request_of = jnp.sum((position[:, None] >= seg_ends[None, :]).astype(jnp.int32), axis=1)
    seg_q = jnp.stack([request_of, position], axis=1)
    seg_k = request_of[None]
    other = lax.ppermute(known, "groups", [(i, (i + 1) % n_groups) for i in range(n_groups)])
    rows = jnp.concatenate([known, known, other, other], axis=0)
    idx_rows = jnp.pad(rows, ((0, 8 - rows.shape[0]), (0, 128 - rows.shape[1])))
    sched = make_schedule(n_dp, requests, per, idx_rows, z)
    queries_here, hop_first, sched = lax.optimization_barrier((queries, hop_first, sched))
    near = attend_near(
        queries_here,
        seg_q,
        seg_k,
        suffix_rotated_key_slots,
        suffix_value_slots,
        shared_prefix_key_slots,
        shared_prefix_value_slots,
    )
    for hop in range(1, n_dp):
        if hop == 1:
            from_below, from_above = hop_first
        else:
            from_below, from_above = below[-1], above[-1]
            if hop == 3:
                from_below, from_above, near = lax.optimization_barrier(
                    (from_below, from_above, near)
                )
            from_below = lax.ppermute(from_below, "dp", up[hop - 1 :])
            from_above = lax.ppermute(from_above, "dp", down[: n_dp - hop])
        below.append(from_below)
        above.append(from_above)

    own = (jnp.transpose(adapter_down_factors, (0, 2, 1)), adapter_up_factors)
    if n_dp > 2:
        sched, below[2], above[2] = lax.optimization_barrier((sched, below[2], above[2]))
    ups, downs, near = adapter_round(sched, own, [], [], requests, n_dp, near)
    attended = attend_far(z, queries, *near, below[1:], above[1:])
    ups, downs, attended = adapter_round(sched, own, ups, downs, requests, n_dp, attended)
    if n_tensor == 4:
        core, chip = by_core(n_tensor), by_chip(n_tensor)

        def share(parts, owners, weigh):
            return project([parts], output_weight_matrix, jnp.stack(owners), n_tensor, PIECES, weigh)

        far = share(attended, (ti ^ 3, ti ^ 2), 8)
        far_other, far_same = far[:PIECES], far[PIECES:]
        far_other, ups, downs = lax.optimization_barrier((far_other, ups, downs))
        from_core = [lax.ppermute(x, "tensor", core) for x in far_other]
        sends = add_all(far_same, from_core)
        sched, sends = lax.optimization_barrier((sched, sends))
        arriving = [lax.ppermute(x, "tensor", chip) for x in sends]
    ups, downs, again = adapter_round(sched, own, ups, downs, requests, n_dp, attended)
    if n_tensor == 4:
        near = share(again, (ti ^ 1, ti), 4)
        near_other, near_same = near[:PIECES], near[PIECES:]
        near_from_core = [lax.ppermute(x, "tensor", core) for x in near_other]
        sched, arriving[:2] = lax.optimization_barrier((sched, arriving[:2]))
    picked = last_adapters(sched, z, own, ups, downs, requests, n_dp)
    if n_tensor == 4:
        picked, arriving[2:-1] = lax.optimization_barrier((picked, arriving[2:-1]))
    rank = picked.shape[1] // 2
    picked_down, picked_up = picked[:, :rank], picked[:, rank:]
    select = request_of[:, None] == jnp.arange(requests, dtype=jnp.int32)[None, :]
    first = lax.dot_general(
        attended,
        picked_down.reshape(-1, width),
        (((1,), (1,)), ((), ())),
        preferred_element_type=F32,
    ).reshape(tokens, requests, -1)
    partial_shrink = jnp.sum(jnp.where(select[:, :, None], first, 0.0), axis=1).astype(BF16)
    if n_tensor == 4:
        bases = [
            mine.astype(F32) + near.astype(F32) + far.astype(F32)
            for mine, near, far in zip(near_same, near_from_core, arriving)
        ]
        base = jnp.concatenate(bases, axis=1)
    else:
        (whole,) = project([attended], output_weight_matrix, jnp.zeros((1,), jnp.int32), 1, 1)
        share = lax.psum_scatter(whole, "tensor", scatter_dimension=1, tiled=True)
        base = share.astype(F32)
    shrink = all_sum(partial_shrink, n_tensor)
    spread = jnp.where(select[:, :, None], shrink[:, None, :], 0).reshape(tokens, -1)
    expand = jnp.dot(
        spread, picked_up.reshape(spread.shape[1], -1), preferred_element_type=F32
    )
    return (base + expand).astype(BF16)


def solution(mesh):
    return jax.shard_map(
        functools.partial(
            per_device, mesh.shape["groups"], mesh.shape["dp"], mesh.shape["tensor"]
        ),
        mesh=mesh,
        in_specs=(
            P(("groups", "dp"), "tensor"),
            P(("groups", "dp"), "tensor"),
            P(("groups", "dp"), "tensor"),
            P(("groups", "dp"), "tensor"),
            P(("groups", "dp"), "tensor"),
            P(("groups", "dp"), None),
            P(("groups", "dp"), None),
            P("tensor", None),
            P("dp", "tensor", None),
            P("dp", None, "tensor"),
        ),
        out_specs=P(("groups", "dp"), "tensor"),
        check_vma=False,
    )
```

```python
import functools
import math

import jax
import jax.numpy as jnp
from jax import lax
from jax.experimental import pallas as pl
from jax.experimental.pallas import tpu as pltpu
from jax.sharding import PartitionSpec as P

HD = 128
CAPS = (2, 2, 2, 1)
PIECES = 4
SMALL = pl.CostEstimate(flops=1, bytes_accessed=1, transcendentals=0)
F32 = jnp.float32
BF16 = jnp.bfloat16
SMEM = pltpu.MemorySpace.SMEM
VMEM = pltpu.MemorySpace.VMEM


def cost(flops):
    return pl.CostEstimate(flops=flops, bytes_accessed=1, transcendentals=0)


def params(mib=32, **more):
    return pltpu.CompilerParams(vmem_limit_bytes=mib * 1024 * 1024, **more)


def attend_block(q, keys, values, bias, factor, peak, summed):
    s = lax.dot_general(q, keys, (((1,), (1,)), ((), ())), preferred_element_type=F32)
    if bias is not None:
        s = s + bias
    high = jnp.max(s, axis=1, keepdims=True)
    high = high if peak is None else jnp.maximum(peak, high)
    w = jnp.exp2((s - high) * factor)
    o = jnp.dot(w.astype(BF16), values, preferred_element_type=F32)
    if peak is not None:
        o = summed * jnp.exp2((peak - high) * factor) + o
    return high, o


def near_kernel(factor, halves, seg_q, seg_k, q_ref, sk_ref, sv_ref, pk_ref, pv_ref, out_ref, stat_ref, bias, both):
    tokens, group = q_ref.shape[0], q_ref.shape[1] // HD

    @pl.when(pl.program_id(0) == 0)
    def _():
        same = seg_q[:, 0:1] == seg_k[0:1, :]
        last = seg_q[:, 1:2]
        where_k = lax.broadcasted_iota(jnp.int32, bias.shape, 1)
        bias[...] = jnp.where(same & (where_k <= last), 0.0, -1e30)
        both[:, HD:] = jnp.ones((both.shape[0], HD), BF16)

    @pl.when(pl.program_id(0) % halves == 0)
    def _():
        both[:tokens, :HD] = sv_ref[...]
        both[tokens:, :HD] = pv_ref[...]

    for h in range(group):
        q = q_ref[:, h * HD : (h + 1) * HD]
        peak, summed = attend_block(q, sk_ref[...], both[:tokens], bias[...], factor, None, None)
        peak, summed = attend_block(q, pk_ref[...], both[tokens:], None, factor, peak, summed)
        at = slice(h * HD, (h + 1) * HD)
        out_ref[:, at] = summed[:, :HD] / summed[:, HD:]
        stat_ref[:, at] = peak * factor + jnp.log2(summed[:, HD:])


def far_kernel(order, factor, halves, place, q_ref, near_ref, stat_ref, *refs):
    hops = len(order)
    below, above = refs[:hops], refs[hops : 2 * hops]
    out_ref, keys, both, held, sems = refs[2 * hops :]
    group = q_ref.shape[1] // HD
    rows = held.shape[1]
    slots = held.shape[2] // (2 * HD)
    slot = pl.program_id(0) // halves

    @pl.when(pl.program_id(0) == 0)
    def _():
        for step, choices in enumerate(order):
            for hop, from_below in sorted(set(choices)):
                here = functools.reduce(
                    jnp.logical_or,
                    [place[0] == i for i, c in enumerate(choices) if c == (hop, from_below)],
                )

                @pl.when(here)
                def _(ref=(below if from_below else above)[hop - 1], to=step):
                    pltpu.make_async_copy(ref, held.at[to], sems.at[to]).start()

        both[:, HD:] = jnp.ones((both.shape[0], HD), BF16)
        for i in range(hops):
            pltpu.make_async_copy(below[0], held.at[i], sems.at[i]).wait()

    @pl.when(pl.program_id(0) % halves == 0)
    def _():
        key_at = pl.ds(pl.multiple_of(slot * HD, HD), HD)
        value_at = pl.ds(pl.multiple_of((slots + slot) * HD, HD), HD)
        for i in range(hops):
            keys[i * rows : (i + 1) * rows] = held[i, :, key_at]
            both[i * rows : (i + 1) * rows, :HD] = held[i, :, value_at]

    for h in range(group):
        at = slice(h * HD, (h + 1) * HD)
        q = q_ref[:, at]
        peak, summed = None, None
        for i in range(hops):
            block = slice(i * rows, (i + 1) * rows)
            peak, summed = attend_block(q, keys[block], both[block], None, factor, peak, summed)
        far, near = jnp.broadcast_to(peak * factor, q.shape), stat_ref[:, at]
        high = jnp.maximum(far, near)
        far, near = jnp.exp2(far - high), jnp.exp2(near - high)
        result = summed[:, :HD] * far + near_ref[:, at] * near
        out_ref[:, at] = (result / (summed[:, HD:] * far + near)).astype(BF16)


FACTOR = math.log2(math.e) / math.sqrt(HD)


def attend_near(q, seg_q, seg_k, keys, values, prefix_keys, prefix_values):
    tokens, width = q.shape
    rows, slots = prefix_keys.shape[0], prefix_keys.shape[1] // HD
    halves = 2 if (width // slots // HD) % 2 == 0 else 1
    wide = width // slots // halves
    part = pl.BlockSpec((tokens, wide), lambda s: (0, s))
    one = lambda n: pl.BlockSpec((n, HD), lambda s: (0, s // halves))
    return pl.pallas_call(
        functools.partial(near_kernel, FACTOR, halves),
        grid=(slots * halves,),
        out_shape=[jax.ShapeDtypeStruct((tokens, width), F32)] * 2,
        in_specs=[
            pl.BlockSpec((tokens, 2), lambda s: (0, 0)),
            pl.BlockSpec((1, tokens), lambda s: (0, 0)),
            part,
            one(tokens),
            one(tokens),
            one(rows),
            one(rows),
        ],
        out_specs=[part] * 2,
        scratch_shapes=[
            pltpu.VMEM((tokens, tokens), F32),
            pltpu.VMEM((tokens + rows, 2 * HD), BF16),
        ],
        compiler_params=params(58),
        cost_estimate=cost(16 * tokens * (tokens + rows) * width),
        name="attend_near",
    )(seg_q, seg_k, q, keys, values, prefix_keys, prefix_values)


def attend_far(z, q, near, stats, below, above):
    tokens, width = q.shape
    rows, hops = below[0].shape[0], len(below)
    slots = below[0].shape[1] // (2 * HD)
    halves = 2 if (width // slots // HD) % 2 == 0 else 1
    part = pl.BlockSpec((tokens, width // slots // halves), lambda s: (0, s))
    anywhere = pl.BlockSpec(memory_space=pl.ANY)
    return pl.pallas_call(
        functools.partial(far_kernel, prefix_order(hops + 1), FACTOR, halves),
        grid=(slots * halves,),
        out_shape=jax.ShapeDtypeStruct((tokens, width), BF16),
        in_specs=[pl.BlockSpec(memory_space=SMEM), part, part, part] + [anywhere] * (2 * hops),
        out_specs=part,
        scratch_shapes=[
            pltpu.VMEM((hops * rows, HD), BF16),
            pltpu.VMEM((hops * rows, 2 * HD), BF16),
            pltpu.VMEM((hops,) + below[0].shape, BF16),
            pltpu.SemaphoreType.DMA((hops,)),
        ],
        compiler_params=params(58),
        cost_estimate=cost(16 * tokens * hops * rows * width),
        name="attend_far",
    )(z, q, near, stats, *below, *above)


def project_kernel(per_tile, wide, n_parts, which, *refs):
    a_refs, w_ref = refs[:n_parts], refs[n_parts]
    outs, done, sems = refs[n_parts + 1 : -2], refs[-2], refs[-1]
    step = pl.program_id(0)
    a = jnp.concatenate([ref[...] for ref in a_refs], axis=1)
    done[step] = jnp.dot(a, w_ref[...], preferred_element_type=F32).astype(BF16)

    def leaving(i):
        piece = done.at[i // per_tile, :, (i % per_tile) * wide : (i % per_tile + 1) * wide]
        return pltpu.make_async_copy(piece, outs[i], sems.at[i])

    for i in range(len(outs)):

        @pl.when(step == i // per_tile)
        def _(i=i):
            leaving(i).start()

    @pl.when(step == pl.num_programs(0) - 1)
    def _():
        for i in range(len(outs)):
            leaving(i).wait()


def project(parts, w, owners, count, pieces, weigh=0):
    rows, depth = parts[0].shape[0], w.shape[0]
    block = w.shape[1] // count
    wide = block // pieces
    tile = max(wide, min(1024, block))
    per_tile, tiles = tile // wide, block // tile
    n = owners.shape[0]
    return pl.pallas_call(
        functools.partial(project_kernel, per_tile, wide, len(parts)),
        out_shape=[jax.ShapeDtypeStruct((rows, wide), BF16)] * (n * pieces),
        grid_spec=pltpu.PrefetchScalarGridSpec(
            num_scalar_prefetch=1,
            grid=(n * tiles,),
            in_specs=[
                *[pl.BlockSpec(a.shape, lambda j, which: (0, 0)) for a in parts],
                pl.BlockSpec((depth, tile), lambda j, which: (0, which[j // tiles] * tiles + j % tiles)),
            ],
            out_specs=[pl.BlockSpec(memory_space=pl.ANY)] * (n * pieces),
            scratch_shapes=[
                pltpu.VMEM((n * tiles, rows, tile), BF16),
                pltpu.SemaphoreType.DMA((n * pieces,)),
            ],
        ),
        compiler_params=params(58),
        cost_estimate=cost(1 + weigh * n * rows * depth * block // 2),
        name="project",
    )(owners, *parts, w)


def add_kernel(n, *refs):
    for a, b, out in zip(refs[:n], refs[n : 2 * n], refs[2 * n :]):
        out[...] = (a[...].astype(F32) + b[...].astype(F32)).astype(BF16)


def add_all(first, second):
    n, (rows, wide) = len(first), first[0].shape
    block = pl.BlockSpec((rows // 2, wide), lambda i: (i, 0))
    return pl.pallas_call(
        functools.partial(add_kernel, n),
        grid=(2,),
        out_shape=[jax.ShapeDtypeStruct((rows, wide), BF16)] * n,
        in_specs=[block] * (2 * n),
        out_specs=[block] * n,
        compiler_params=params(58),
        cost_estimate=SMALL,
        name="add_all",
    )(*first, *second)


def most_slots(n_dp, requests):
    return sum(CAPS) + requests * (n_dp - 1) + n_dp


def schedule_kernel(n_dp, requests, per, idx_ref, z_ref, out_ref):
    limit = most_slots(n_dp, requests)
    links = n_dp - 1
    idx = idx_ref[...]
    shape = idx.shape
    z = z_ref[0]
    lane = lax.broadcasted_iota(jnp.int32, shape, 1)
    row = lax.broadcasted_iota(jnp.int32, shape, 0)
    link = lax.broadcasted_iota(jnp.int32, (links,) + shape, 0)
    valid = (lane < n_dp * requests) & (row < 4)
    down = (row % 2) == 1
    taker = (z + n_dp - lane // requests) % n_dp
    holder = idx // per
    local = idx % per
    own = valid & (taker == holder)
    dst = jnp.where(down, n_dp - 1 - taker, taker)
    src = jnp.where(down, n_dp - 1 - holder, holder)
    me = jnp.where(down, n_dp - 1 - z, z)
    moving = valid & (src < dst)
    dst = jnp.where(moving, dst, 0)
    pos = jnp.where(moving, src, 0)
    rank = dst * 256 + 255 - (taker * requests + lane % requests)
    zero = jnp.zeros(shape, jnp.int32)

    def one_round(first, slots, pos, came, codes):
        can = (pos[None] == link) & (dst[None] > link)
        code = jnp.where(src == me, local, per + came)
        moved = zero
        for slot in range(slots):
            key = jnp.where(can, rank[None], -1)
            best = jnp.max(key, axis=2, keepdims=True)
            chosen = can & (key == best)
            can = can & ~chosen
            sent = jnp.sum(jnp.where(chosen & (link == me[None]), code[None], 0), axis=0)
            codes = jnp.where(lane == first + slot, jnp.sum(sent, axis=1, keepdims=True), codes)
            got = jnp.sum(jnp.where(chosen & (link + 1 == me[None]), 1, 0), axis=0)
            came = jnp.where(got > 0, first + slot, came)
            moved = moved + jnp.sum(jnp.where(chosen, 1, 0), axis=0)
        return pos + moved, came, codes

    came, codes = zero, zero
    first = 0

    def left(pos):
        return jnp.max(jnp.where(pos < dst, 1, 0))

    unfinished = []
    for slots in CAPS:
        unfinished.append(left(pos))
        pos, came, codes = one_round(first, slots, pos, came, codes)
        first += slots

    def later(carry):
        k, _, pos, came, codes = carry
        pos, came, codes = one_round(k, 1, pos, came, codes)
        return k + 1, left(pos), pos, came, codes

    used, _, _, came, codes = lax.while_loop(
        lambda c: (c[1] > 0) & (c[0] < limit), later, (jnp.int32(first), left(pos), pos, came, codes)
    )
    used = jnp.where(unfinished[-1] > 0, used, first - CAPS[-1])
    place = jnp.where(own & (row == 0), local, 0)
    place = place + jnp.where(moving & (row == 0), per + came, 0)
    place = place + jnp.where(moving & (row == 1), per + limit + came, 0)
    place = jnp.sum(jnp.where(row < 2, place, 0), axis=0, keepdims=True)
    out = jnp.where(row < 2, codes, 0)
    out = jnp.where(row == 2, place, out)
    out_ref[...] = jnp.where(row == 3, used, out)


def make_schedule(n_dp, requests, per, idx_rows, z):
    return pl.pallas_call(
        functools.partial(schedule_kernel, n_dp, requests, per),
        out_shape=jax.ShapeDtypeStruct((8, 128), jnp.int32),
        in_specs=[pl.BlockSpec(memory_space=VMEM), pl.BlockSpec(memory_space=SMEM)],
        out_specs=pl.BlockSpec(memory_space=VMEM),
        cost_estimate=SMALL,
        name="schedule",
    )(idx_rows, z)


def slots_of(came):
    return [(r, j) for r, ref in enumerate(came) for j in range(CAPS[r])]


def fetch(code, per, own, ups, downs, limit, out, sems):
    rank = own[0].shape[1]

    @pl.when(code < per)
    def _():
        at = jnp.minimum(code, per - 1)
        for half in range(2):
            to = out.at[half * rank : (half + 1) * rank]
            pltpu.make_async_copy(own[half].at[at], to, sems.at[half]).start()

    for base, came in ((per, ups), (per + limit, downs)):
        for k, (r, j) in enumerate(slots_of(came)):

            @pl.when(code == base + k)
            def _(ref=came[r], j=j):
                for half in range(2):
                    part = slice(half * rank, (half + 1) * rank)
                    pltpu.make_async_copy(ref.at[j, part], out.at[part], sems.at[half]).start()


def fetched(own, out, sems):
    rank = own[0].shape[1]
    for half in range(2):
        to = out.at[half * rank : (half + 1) * rank]
        pltpu.make_async_copy(own[half].at[0], to, sems.at[half]).wait()


def pick_kernel(first, count, per, limit, n_came, sched, down_ref, up_ref, *refs):
    ups, downs = refs[:n_came], refs[n_came : 2 * n_came]
    outs, sems = refs[2 * n_came : -1], refs[-1]
    own = (down_ref, up_ref)
    for i in range(count):
        for way, came in enumerate((ups, downs)):
            code = sched[way, first + i]
            fetch(code, per, own, came, (), limit, outs[way].at[i], sems.at[way, i])
    for i in range(count):
        for way in range(2):
            fetched(own, outs[way].at[i], sems.at[way, i])


def slot_shape(own):
    return (2 * own[0].shape[1], own[0].shape[2])


def pick_sends(sched, own, ups, downs, number, limit):
    count, first = CAPS[number], sum(CAPS[:number])
    anywhere = pl.BlockSpec(memory_space=pl.ANY)
    in_vmem = pl.BlockSpec(memory_space=VMEM)
    out = jax.ShapeDtypeStruct((count,) + slot_shape(own), BF16)
    return pl.pallas_call(
        functools.partial(pick_kernel, first, count, own[0].shape[0], limit, len(ups)),
        out_shape=[out] * 2,
        in_specs=[pl.BlockSpec(memory_space=SMEM)] + [anywhere] * (2 + 2 * len(ups)),
        out_specs=[in_vmem] * 2,
        scratch_shapes=[pltpu.SemaphoreType.DMA((2, count, 2))],
        compiler_params=params(16),
        cost_estimate=SMALL,
        name="pick",
    )(sched, *own, *ups, *downs)


def gather_kernel(per, limit, requests, n_came, sched, z, down_ref, up_ref, *refs):
    ups, downs = refs[:n_came], refs[n_came : 2 * n_came]
    out, sems = refs[-2], refs[-1]
    own = (down_ref, up_ref)
    for r in range(requests):
        code = sched[2, r]
        fetch(code, per, own, ups, downs, limit, out.at[r], sems.at[r])
    for r in range(requests):
        fetched(own, out.at[r], sems.at[r])


def gather_own(sched, z, own, ups, downs, requests, limit):
    anywhere = pl.BlockSpec(memory_space=pl.ANY)
    return pl.pallas_call(
        functools.partial(gather_kernel, own[0].shape[0], limit, requests, len(ups)),
        out_shape=jax.ShapeDtypeStruct((requests,) + slot_shape(own), BF16),
        in_specs=[pl.BlockSpec(memory_space=SMEM)] * 2 + [anywhere] * (2 + 2 * len(ups)),
        out_specs=pl.BlockSpec(memory_space=VMEM),
        scratch_shapes=[pltpu.SemaphoreType.DMA((requests, 2))],
        compiler_params=params(16),
        cost_estimate=SMALL,
        name="gather_own",
    )(sched, z, *own, *ups, *downs)


def later_rounds(sched, z, own, ups, downs, requests, limit, n_dp):
    up, down = line(n_dp)
    per = own[0].shape[0]
    made = sum(CAPS)
    spare = jnp.zeros((limit - made,) + slot_shape(own), BF16)
    up_all = jnp.concatenate([*ups, spare])
    down_all = jnp.concatenate([*downs, spare])

    def choose(code, came):
        at = jnp.minimum(code, per - 1)
        held = [lax.dynamic_index_in_dim(o, at, 0, keepdims=False) for o in own]
        passed = lax.dynamic_index_in_dim(came, jnp.clip(code - per, 0, limit - 1), 0, keepdims=False)
        return jnp.where(code < per, jnp.concatenate(held), passed)

    def step(carry):
        k, up_all, down_all = carry
        from_below = lax.ppermute(choose(sched[0, k], up_all), "dp", up)
        from_above = lax.ppermute(choose(sched[1, k], down_all), "dp", down)
        up_all = lax.dynamic_update_index_in_dim(up_all, from_below, k, 0)
        down_all = lax.dynamic_update_index_in_dim(down_all, from_above, k, 0)
        return k + 1, up_all, down_all

    _, up_all, down_all = lax.while_loop(
        lambda c: c[0] < sched[3, 0], step, (jnp.int32(made), up_all, down_all)
    )
    places = sched[2]
    picked = []
    for r in range(requests):
        code = places[r]
        below = choose(code, up_all)
        above = lax.dynamic_index_in_dim(
            down_all, jnp.clip(code - per - limit, 0, limit - 1), 0, keepdims=False
        )
        picked.append(jnp.where(code >= per + limit, above, below))
    return jnp.stack(picked)


def line(n):
    return [(i, i + 1) for i in range(n - 1)], [(i + 1, i) for i in range(n - 1)]


def adapter_round(sched, own, ups, downs, requests, n_dp, after=None):
    up, down = line(n_dp)
    sends = pick_sends(sched, own, ups, downs, len(ups), most_slots(n_dp, requests))
    sends, after = lax.optimization_barrier((sends, after))
    ups = ups + [lax.ppermute(sends[0], "dp", up)]
    downs = downs + [lax.ppermute(sends[1], "dp", down)]
    return ups, downs, after


def last_adapters(sched, z, own, ups, downs, requests, n_dp):
    limit = most_slots(n_dp, requests)

    def one_round():
        return adapter_round(sched, own, ups, downs, requests, n_dp)[:2]

    def enough():
        return gather_own(sched, z, own, ups, downs, requests, limit)

    def one_more():
        return gather_own(sched, z, own, *one_round(), requests, limit)

    def many_more():
        return later_rounds(sched, z, own, *one_round(), requests, limit, n_dp)

    used = sched[3, 0]
    short = (used > sum(CAPS[:-1])).astype(jnp.int32) + (used > sum(CAPS)).astype(jnp.int32)
    return lax.switch(short, (enough, one_more, many_more))


def by_core(n):
    return [(i, i ^ 1) for i in range(n)]


def by_chip(n):
    return [(i, i ^ 2) for i in range(n)]


def added(a, b):
    return (a.astype(F32) + b.astype(F32)).astype(BF16)


def all_sum(x, n_tensor):
    if n_tensor != 4:
        return lax.psum(x, "tensor")
    x = added(x, lax.ppermute(x, "tensor", by_core(n_tensor)))
    return added(x, lax.ppermute(x, "tensor", by_chip(n_tensor)))


def prefix_order(n):
    table = []
    for z in range(n):
        seen = []
        for hop in range(1, n):
            seen += [(hop, True)] if hop <= z else []
            seen += [(hop, False)] if hop <= n - 1 - z else []
        table.append(seen)
    return [[table[z][s] for z in range(n)] for s in range(n - 1)]


def per_device(
    n_groups,
    n_dp,
    n_tensor,
    queries,
    suffix_rotated_key_slots,
    suffix_value_slots,
    shared_prefix_key_slots,
    shared_prefix_value_slots,
    lengths,
    request_adapter_index,
    output_weight_matrix,
    adapter_down_factors,
    adapter_up_factors,
):
    tokens, width = queries.shape
    requests = lengths.shape[1]
    per = adapter_down_factors.shape[0]
    zi = lax.axis_index("dp").astype(jnp.int32)
    z = zi.reshape(1)
    ti = lax.axis_index("tensor").astype(jnp.int32)
    up, down = line(n_dp)

    own_rows = jnp.concatenate([shared_prefix_key_slots, shared_prefix_value_slots], axis=1)
    below, above = [own_rows], [own_rows]

    known = jnp.concatenate(
        [request_adapter_index]
        + [
            lax.ppermute(request_adapter_index, "dp", [(i, (i + s) % n_dp) for i in range(n_dp)])
            for s in range(1, n_dp)
        ],
        axis=1,
    )

    own_rows, known = lax.optimization_barrier((own_rows, known))
    below, above = [own_rows], [own_rows]
    hop_first = (lax.ppermute(own_rows, "dp", up), lax.ppermute(own_rows, "dp", down))

    position = jnp.arange(tokens, dtype=jnp.int32)
    seg_ends = jnp.cumsum(lengths[0])
    request_of = jnp.sum((position[:, None] >= seg_ends[None, :]).astype(jnp.int32), axis=1)
    seg_q = jnp.stack([request_of, position], axis=1)
    seg_k = request_of[None]
    other = lax.ppermute(known, "groups", [(i, (i + 1) % n_groups) for i in range(n_groups)])
    rows = jnp.concatenate([known, known, other, other], axis=0)
    idx_rows = jnp.pad(rows, ((0, 8 - rows.shape[0]), (0, 128 - rows.shape[1])))
    sched = make_schedule(n_dp, requests, per, idx_rows, z)
    queries_here, hop_first, sched = lax.optimization_barrier((queries, hop_first, sched))
    near = attend_near(
        queries_here,
        seg_q,
        seg_k,
        suffix_rotated_key_slots,
        suffix_value_slots,
        shared_prefix_key_slots,
        shared_prefix_value_slots,
    )
    for hop in range(1, n_dp):
        if hop == 1:
            from_below, from_above = hop_first
        else:
            from_below, from_above = below[-1], above[-1]
            if hop == 3:
                from_below, from_above, near = lax.optimization_barrier(
                    (from_below, from_above, near)
                )
            from_below = lax.ppermute(from_below, "dp", up[hop - 1 :])
            from_above = lax.ppermute(from_above, "dp", down[: n_dp - hop])
        below.append(from_below)
        above.append(from_above)

    own = (jnp.transpose(adapter_down_factors, (0, 2, 1)), adapter_up_factors)
    if n_dp > 2:
        sched, below[2], above[2] = lax.optimization_barrier((sched, below[2], above[2]))
    ups, downs, near = adapter_round(sched, own, [], [], requests, n_dp, near)
    attended = attend_far(z, queries, *near, below[1:], above[1:])
    ups, downs, attended = adapter_round(sched, own, ups, downs, requests, n_dp, attended)
    if n_tensor == 4:
        core, chip = by_core(n_tensor), by_chip(n_tensor)

        def share(parts, owners, weigh):
            return project([parts], output_weight_matrix, jnp.stack(owners), n_tensor, PIECES, weigh)

        far = share(attended, (ti ^ 3, ti ^ 2), 8)
        far_other, far_same = far[:PIECES], far[PIECES:]
        far_other, ups, downs = lax.optimization_barrier((far_other, ups, downs))
        from_core = [lax.ppermute(x, "tensor", core) for x in far_other]
        sends = add_all(far_same, from_core)
        sched, sends = lax.optimization_barrier((sched, sends))
        arriving = [lax.ppermute(x, "tensor", chip) for x in sends]
    ups, downs, again = adapter_round(sched, own, ups, downs, requests, n_dp, attended)
    if n_tensor == 4:
        near = share(again, (ti ^ 1, ti), 4)
        near_other, near_same = near[:PIECES], near[PIECES:]
        near_from_core = [lax.ppermute(x, "tensor", core) for x in near_other]
        sched, arriving[:2] = lax.optimization_barrier((sched, arriving[:2]))
    picked = last_adapters(sched, z, own, ups, downs, requests, n_dp)
    if n_tensor == 4:
        picked, arriving[2:-1] = lax.optimization_barrier((picked, arriving[2:-1]))
    rank = picked.shape[1] // 2
    picked_down, picked_up = picked[:, :rank], picked[:, rank:]
    select = request_of[:, None] == jnp.arange(requests, dtype=jnp.int32)[None, :]
    first = lax.dot_general(
        attended,
        picked_down.reshape(-1, width),
        (((1,), (1,)), ((), ())),
        preferred_element_type=F32,
    ).reshape(tokens, requests, -1)
    partial_shrink = jnp.sum(jnp.where(select[:, :, None], first, 0.0), axis=1).astype(BF16)
    if n_tensor == 4:
        bases = [
            mine.astype(F32) + near.astype(F32) + far.astype(F32)
            for mine, near, far in zip(near_same, near_from_core, arriving)
        ]
        base = jnp.concatenate(bases, axis=1)
    else:
        (whole,) = project([attended], output_weight_matrix, jnp.zeros((1,), jnp.int32), 1, 1)
        share = lax.psum_scatter(whole, "tensor", scatter_dimension=1, tiled=True)
        base = share.astype(F32)
    shrink = all_sum(partial_shrink, n_tensor)
    spread = jnp.where(select[:, :, None], shrink[:, None, :], 0).reshape(tokens, -1)
    expand = jnp.dot(
        spread, picked_up.reshape(spread.shape[1], -1), preferred_element_type=F32
    )
    return (base + expand).astype(BF16)


def solution(mesh):
    return jax.shard_map(
        functools.partial(
            per_device, mesh.shape["groups"], mesh.shape["dp"], mesh.shape["tensor"]
        ),
        mesh=mesh,
        in_specs=(
            P(("groups", "dp"), "tensor"),
            P(("groups", "dp"), "tensor"),
            P(("groups", "dp"), "tensor"),
            P(("groups", "dp"), "tensor"),
            P(("groups", "dp"), "tensor"),
            P(("groups", "dp"), None),
            P(("groups", "dp"), None),
            P("tensor", None),
            P("dp", "tensor", None),
            P("dp", None, "tensor"),
        ),
        out_specs=P(("groups", "dp"), "tensor"),
        check_vma=False,
    )
```
